32 devices in a mesh: dp: 4 (over z), fsdp: 8 (over y, x, core).
Axes of the slice: x: 2, y: 2, z: 4, core: 2. Of those that a mesh axis runs over, the one named last changes fastest.
Arguments:
- tokens: bfloat16 [8192, 2048], P(('dp', 'fsdp')), may hold values from -6 to 6
- positions: int32 [8192], P(('dp', 'fsdp')), may hold values from -1 to 255, as said below
- cotangent: bfloat16 [8192, 2048], P(('dp', 'fsdp')), may hold values from -6 to 6
- entry_weight: float32 [3, 2048, 2048], P(None, ('dp', 'fsdp')), may hold values from -0.125 to 0.125
- mixing_weight: float32 [1, 2048, 2048], P(None, ('dp', 'fsdp')), may hold values from -0.5 to 0.5
- attention_gain: float32 [1, 2048], P(None, ('dp', 'fsdp')), may hold values from 0.5 to 1.5
- expand_weight: float32 [2, 8192, 2048], P(None, ('dp', 'fsdp')), may hold values from -0.125 to 0.125
- shrink_weight: float32 [1, 2048, 8192], P(None, ('dp', 'fsdp')), may hold values from -0.0625 to 0.0625
- feedforward_gain: float32 [1, 2048], P(None, ('dp', 'fsdp')), may hold values from 0.5 to 1.5
- entry_moment: float32 [3, 2048, 2048], P(None, ('dp', 'fsdp'))
- entry_square: float32 [3, 2048, 2048], P(None, ('dp', 'fsdp')), may hold values from 1024 to 4096
- mixing_moment: float32 [1, 2048, 2048], P(None, ('dp', 'fsdp'))
- mixing_square: float32 [1, 2048, 2048], P(None, ('dp', 'fsdp')), may hold values from 10 to 42
- attention_moment: float32 [1, 2048], P(None, ('dp', 'fsdp'))
- attention_square: float32 [1, 2048], P(None, ('dp', 'fsdp')), may hold values from 512 to 2048
- expand_moment: float32 [2, 8192, 2048], P(None, ('dp', 'fsdp'))
- expand_square: float32 [2, 8192, 2048], P(None, ('dp', 'fsdp')), may hold values from 10 to 42
- shrink_moment: float32 [1, 2048, 8192], P(None, ('dp', 'fsdp'))
- shrink_square: float32 [1, 2048, 8192], P(None, ('dp', 'fsdp')), may hold values from 51 to 204
- feedforward_moment: float32 [1, 2048], P(None, ('dp', 'fsdp'))
- feedforward_square: float32 [1, 2048], P(None, ('dp', 'fsdp')), may hold values from 102 to 409
Outputs:
- layer_output: bfloat16 [8192, 2048], P(('dp', 'fsdp'))
- input_gradient: float32 [8192, 2048], P(('dp', 'fsdp'))
- entry_gradient: float32 [3, 2048, 2048], P(None, ('dp', 'fsdp'))
- mixing_gradient: float32 [1, 2048, 2048], P(None, ('dp', 'fsdp'))
- attention_gradient: float32 [1, 2048], P(None, ('dp', 'fsdp'))
- expand_gradient: float32 [2, 8192, 2048], P(None, ('dp', 'fsdp'))
- shrink_gradient: float32 [1, 2048, 8192], P(None, ('dp', 'fsdp'))
- feedforward_gradient: float32 [1, 2048], P(None, ('dp', 'fsdp'))
- entry_updated: float32 [3, 2048, 2048], P(None, ('dp', 'fsdp'))
- mixing_updated: float32 [1, 2048, 2048], P(None, ('dp', 'fsdp'))
- attention_updated: float32 [1, 2048], P(None, ('dp', 'fsdp'))
- expand_updated: float32 [2, 8192, 2048], P(None, ('dp', 'fsdp'))
- shrink_updated: float32 [1, 2048, 8192], P(None, ('dp', 'fsdp'))
- feedforward_updated: float32 [1, 2048], P(None, ('dp', 'fsdp'))
- entry_momentum: float32 [3, 2048, 2048], P(None, ('dp', 'fsdp'))
- entry_variance: float32 [3, 2048, 2048], P(None, ('dp', 'fsdp'))
- mixing_momentum: float32 [1, 2048, 2048], P(None, ('dp', 'fsdp'))
- mixing_variance: float32 [1, 2048, 2048], P(None, ('dp', 'fsdp'))
- attention_momentum: float32 [1, 2048], P(None, ('dp', 'fsdp'))
- attention_variance: float32 [1, 2048], P(None, ('dp', 'fsdp'))
- expand_momentum: float32 [2, 8192, 2048], P(None, ('dp', 'fsdp'))
- expand_variance: float32 [2, 8192, 2048], P(None, ('dp', 'fsdp'))
- shrink_momentum: float32 [1, 2048, 8192], P(None, ('dp', 'fsdp'))
- shrink_variance: float32 [1, 2048, 8192], P(None, ('dp', 'fsdp'))
- feedforward_momentum: float32 [1, 2048], P(None, ('dp', 'fsdp'))
- feedforward_variance: float32 [1, 2048], P(None, ('dp', 'fsdp'))
The draws below stay inside these ranges and needn't reach their ends.
Inputs may be any that keep to these rules, and one draw needn't show every extreme that they name: Each device's 256 slots hold whole sequences packed from its first slot, positions counting 0, 1, 2 within each; the remaining slots are -1. Some device holds a single sequence of all 256 slots; every other device has at least one empty slot.
All inputs are finite; a program needn't handle non-finite values.
Results may differ from the reference program's by a relative error of at most 0.015.
The reference program's roundings to bfloat16 on the way count: a program that leaves them out, or rounds other values in their place, can miss the bound.
Values may be sent and summed in bfloat16 or wider, within the bound.
No kernel may reach another device: no remote copies, remote signals or barrier semaphores. Data moves between devices by JAX's collectives and lax.ppermute only.
A program may use at most 576 MiB of HBM per device.

```python
import math
import jax
import jax.numpy as jnp
from jax import lax

D = 2048
HEADS = 32
HEAD = 64
FF = 8192
CAP = 256
STEP = 3
TOKENS = 8192


def draw_positions(key, part):
    flag_key, count_key, full_key = jax.random.split(key, 3)
    devices = TOKENS // CAP
    slots = jnp.arange(CAP, dtype=jnp.int32)
    starts = (jax.random.randint(flag_key, (devices, CAP), 0, 96) == 0) | (slots[None, :] == 0)
    begin = lax.cummax(jnp.where(starts, slots[None, :], 0), axis=1)
    within = slots[None, :] - begin
    counts = jax.random.randint(count_key, (devices, 1), CAP // 4, CAP)
    chosen = jax.random.randint(full_key, (), 0, devices)
    full = jnp.arange(devices, dtype=jnp.int32)[:, None] == chosen
    within = jnp.where(full, jnp.broadcast_to(slots[None, :], (devices, CAP)), within)
    live = full | (slots[None, :] < counts)
    return jnp.where(live, within, -1).reshape(-1).astype(jnp.int32)


def moment_draw(key, shape, level):
    scale = level * jnp.sqrt(jnp.float32(TOKENS))
    return jnp.clip(jax.random.normal(key, shape, jnp.float32), -6.0, 6.0) * scale


def draw_entry_moment(key, part):
    return moment_draw(jax.random.fold_in(key, 11), (3, D, D), 0.8)


def draw_mixing_moment(key, part):
    return moment_draw(jax.random.fold_in(key, 12), (1, D, D), 0.075)


def draw_attention_moment(key, part):
    return moment_draw(jax.random.fold_in(key, 13), (1, D), 0.5)


def draw_expand_moment(key, part):
    return moment_draw(jax.random.fold_in(key, 14), (2, FF, D), 0.075)


def draw_shrink_moment(key, part):
    return moment_draw(jax.random.fold_in(key, 15), (1, D, FF), 0.16)


def draw_feedforward_moment(key, part):
    return moment_draw(jax.random.fold_in(key, 16), (1, D), 0.23)


def shard_levels(stream_key, extent, cuts, least, high):
    def one(dim, blocks):
        heights = jax.random.uniform(jax.random.fold_in(jax.random.fold_in(stream_key, 6), dim), (blocks,), jnp.float32, least / len(cuts), high / len(cuts))
        return jnp.repeat(jnp.exp(heights), extent[dim] // blocks).reshape((-1,) + (1,) * (len(extent) - dim - 1))

    level = one(*cuts[0])
    for cut in cuts[1:]:
        level = level * one(*cut)
    return level


def normal_values(rng, extent, deviation, limit, cuts=(), held_as=jnp.bfloat16):
    result = deviation * jax.random.normal(rng, extent, jnp.float32)
    if cuts:
        result = result * shard_levels(rng, extent, cuts, -0.22, 0.18)
    return jnp.clip(result, -limit, limit).astype(held_as)


def setup_inputs(seed: int = 0) -> dict:
    seeds = jax.random.split(jax.random.key(seed), 22)
    return {
        "tokens": normal_values(seeds[0], (TOKENS, D), 1.0, 6.0, ((0, 32),)),
        "positions": draw_positions(jax.random.fold_in(seeds[21], 71), 0),
        "cotangent": normal_values(seeds[2], (TOKENS, D), 1.0, 6.0, ((0, 32),)),
        "entry_weight": normal_values(seeds[3], (3, D, D), D ** -0.5, 0.125, ((1, 32),), jnp.float32),
        "mixing_weight": normal_values(seeds[4], (1, D, D), (D // 16) ** -0.5, 0.5, ((1, 32),), jnp.float32),
        "attention_gain": jnp.clip(1.0 + 0.1 * jax.random.normal(seeds[5], (1, D), jnp.float32), 0.5, 1.5),
        "expand_weight": normal_values(seeds[6], (2, FF, D), D ** -0.5, 0.125, ((1, 32),), jnp.float32),
        "shrink_weight": normal_values(seeds[7], (1, D, FF), FF ** -0.5, 0.0625, ((1, 32),), jnp.float32),
        "feedforward_gain": jnp.clip(1.0 + 0.1 * jax.random.normal(seeds[8], (1, D), jnp.float32), 0.5, 1.5),
        "entry_moment": draw_entry_moment(jax.random.fold_in(seeds[21], 71), 0),
        "entry_square": jnp.clip(jnp.exp(math.log(4096.0) - 1.3862944 * jax.random.uniform(seeds[10], (3, D, D), jnp.float32) ** shard_levels(seeds[10], (3, D, D), ((1, 32),), -0.2, 0.2)), 1024.0, 4096.0),
        "mixing_moment": draw_mixing_moment(jax.random.fold_in(seeds[21], 71), 0),
        "mixing_square": jnp.clip(jnp.exp(math.log(42.0) - 1.43508453 * jax.random.uniform(seeds[12], (1, D, D), jnp.float32) ** shard_levels(seeds[12], (1, D, D), ((1, 32),), -0.2, 0.2)), 10.0, 42.0),
        "attention_moment": draw_attention_moment(jax.random.fold_in(seeds[21], 71), 0),
        "attention_square": jnp.clip(jnp.exp(math.log(2048.0) - 1.3862944 * jax.random.uniform(seeds[14], (1, D), jnp.float32) ** shard_levels(seeds[14], (1, D), ((1, 32),), -0.2, 0.2)), 512.0, 2048.0),
        "expand_moment": draw_expand_moment(jax.random.fold_in(seeds[21], 71), 0),
        "expand_square": jnp.clip(jnp.exp(math.log(42.0) - 1.43508453 * jax.random.uniform(seeds[16], (2, FF, D), jnp.float32) ** shard_levels(seeds[16], (2, FF, D), ((1, 32),), -0.2, 0.2)), 10.0, 42.0),
        "shrink_moment": draw_shrink_moment(jax.random.fold_in(seeds[21], 71), 0),
        "shrink_square": jnp.clip(jnp.exp(math.log(204.0) - 1.3862944 * jax.random.uniform(seeds[18], (1, D, FF), jnp.float32) ** shard_levels(seeds[18], (1, D, FF), ((1, 32),), -0.2, 0.2)), 51.0, 204.0),
        "feedforward_moment": draw_feedforward_moment(jax.random.fold_in(seeds[21], 71), 0),
        "feedforward_square": jnp.clip(jnp.exp(math.log(409.0) - 1.3887423 * jax.random.uniform(seeds[20], (1, D), jnp.float32) ** shard_levels(seeds[20], (1, D), ((1, 32),), -0.2, 0.2)), 102.0, 409.0),
    }


@jax.custom_vjp
def low(v):
    return lax.optimization_barrier(v.astype(jnp.bfloat16)).astype(jnp.float32)

@jax.custom_vjp
def low_back(v):
    return v

def low_keep(v):
    return (low(v), None)

def low_pass(kept, grad):
    return (grad,)

def back_keep(v):
    return (v, None)

def back_low(kept, grad):
    return (low(grad),)
low.defvjp(low_keep, low_pass)
low_back.defvjp(back_keep, back_low)
EPS = 1e-05
THETA = 130000.0
RATE = 0.01
MIXING_RATE = 0.04
GAIN_RATE = 0.3
BETA_ONE = 0.9
BETA_TWO = 0.95
ADAM_EPS = 1e-08
DECAY = 0.1
HIGH = lax.Precision.HIGHEST

def project(left, weight):
    return jnp.dot(left, weight.T, precision=HIGH, preferred_element_type=jnp.float32)

def norm_rows(value, gain):
    return value * lax.rsqrt(lax.optimization_barrier(jnp.mean(value * value, axis=-1, keepdims=True)) + EPS) * gain

def rope_tables(positions):
    half = HEAD // 2
    freq = THETA ** (-2.0 * jnp.arange(half, dtype=jnp.float32) / HEAD)
    angle = positions.astype(jnp.float32)[:, None] * freq[None, :]
    return (jnp.cos(angle), jnp.sin(angle))

def rotate(value, cosine, sine):
    half = HEAD // 2
    shaped = value.reshape(value.shape[0], HEADS, HEAD)
    first = shaped[..., :half]
    second = shaped[..., half:]
    cos_rows = cosine[:, None, :]
    sin_rows = sine[:, None, :]
    joined = jnp.concatenate([first * cos_rows - second * sin_rows, second * cos_rows + first * sin_rows], axis=-1)
    return joined.reshape(value.shape)

def attend(pieces):
    query, keys, values, places = pieces
    slots = jnp.arange(CAP, dtype=jnp.int32)
    same = places[:, None] - places[None, :] == slots[:, None] - slots[None, :]
    visible = same & (slots[None, :] <= slots[:, None])
    query_heads = query.reshape(CAP, HEADS, HEAD)
    key_heads = keys.reshape(CAP, HEADS, HEAD)
    value_heads = values.reshape(CAP, HEADS, HEAD)
    scores = jnp.einsum('qhd,khd->hqk', query_heads, key_heads, precision=HIGH) * HEAD ** (-0.5)
    scores = low_back(scores)
    scores = jnp.where(visible[None], scores, -1e+30)
    top = lax.optimization_barrier(jnp.max(scores, axis=-1, keepdims=True))
    weights = jnp.exp(scores - top)
    probs = low(weights / lax.optimization_barrier(jnp.sum(weights, axis=-1, keepdims=True)))
    return jnp.einsum('hqk,khd->qhd', probs, value_heads, precision=HIGH).reshape(CAP, D)

def forward(inputs, positions, entry, mixing, attention, expand, shrink, feedforward):
    cosine, sine = rope_tables(positions)
    normed = low(norm_rows(inputs, low(attention)[0]))
    mixed = low_back(project(normed, low(entry).reshape(3 * D, D)))
    query = low(rotate(mixed[:, :D], cosine, sine))
    keys = low(rotate(mixed[:, D:2 * D], cosine, sine))
    values = low(mixed[:, 2 * D:])
    blocks = lax.map(jax.checkpoint(attend), (query.reshape(-1, CAP, D), keys.reshape(-1, CAP, D), values.reshape(-1, CAP, D), positions.reshape(-1, CAP)))
    attended = low_back(low(blocks.reshape(-1, D)))
    middle = inputs + low_back(project(attended, low(mixing)[0]))
    normed_two = low(norm_rows(middle, low(feedforward)[0]))
    both = low_back(project(normed_two, low(expand).reshape(2 * FF, D)))
    gate = both[:, :FF]
    upward = both[:, FF:]
    hidden = low(jax.nn.silu(gate) * upward)
    return middle + low_back(project(hidden, low(shrink)[0]))

def adamw(weight, gradient, moment, square, rate, decay):
    moment_new = BETA_ONE * moment + (1.0 - BETA_ONE) * gradient
    square_new = BETA_TWO * square + (1.0 - BETA_TWO) * gradient * gradient
    corrected = moment_new / (1.0 - BETA_ONE ** STEP)
    spread = jnp.sqrt(square_new / (1.0 - BETA_TWO ** STEP)) + ADAM_EPS
    return (weight - rate * (corrected / spread + decay * weight), moment_new, square_new)

def reference(tokens, positions, cotangent, entry_weight, mixing_weight, attention_gain, expand_weight, shrink_weight, feedforward_gain, entry_moment, entry_square, mixing_moment, mixing_square, attention_moment, attention_square, expand_moment, expand_square, shrink_moment, shrink_square, feedforward_moment, feedforward_square):
    inputs = tokens.astype(jnp.float32)
    live = (positions >= 0).astype(jnp.float32)[:, None]

    def run(inputs, entry, mixing, attention, expand, shrink, feedforward):
        return forward(inputs, positions, entry, mixing, attention, expand, shrink, feedforward)
    output, pull = jax.vjp(run, inputs, entry_weight, mixing_weight, attention_gain, expand_weight, shrink_weight, feedforward_gain)
    grads = pull(cotangent.astype(jnp.float32) * live)
    entry_new = adamw(entry_weight, grads[1], entry_moment, entry_square, RATE, DECAY)
    mixing_new = adamw(mixing_weight, grads[2], mixing_moment, mixing_square, MIXING_RATE, DECAY)
    attention_new = adamw(attention_gain, grads[3], attention_moment, attention_square, GAIN_RATE, 0.0)
    expand_new = adamw(expand_weight, grads[4], expand_moment, expand_square, RATE, DECAY)
    shrink_new = adamw(shrink_weight, grads[5], shrink_moment, shrink_square, RATE, DECAY)
    feedforward_new = adamw(feedforward_gain, grads[6], feedforward_moment, feedforward_square, GAIN_RATE, 0.0)
    return (output.astype(jnp.bfloat16), grads[0], grads[1], grads[2], grads[3], grads[4], grads[5], grads[6], entry_new[0], mixing_new[0], attention_new[0], expand_new[0], shrink_new[0], feedforward_new[0], entry_new[1], entry_new[2], mixing_new[1], mixing_new[2], attention_new[1], attention_new[2], expand_new[1], expand_new[2], shrink_new[1], shrink_new[2], feedforward_new[1], feedforward_new[2])
```

```python
import functools
import jax
import jax.numpy as jnp
from jax import lax
from jax.sharding import PartitionSpec as P

HEADS = 32
HEAD = 64
STEP = 3


EPS = 1e-05
THETA = 130000.0
RATE = 0.01
MIXING_RATE = 0.04
GAIN_RATE = 0.3
BETA_ONE = 0.9
BETA_TWO = 0.95
ADAM_EPS = 1e-08
DECAY = 0.1


def contract_last(left, right):
    return lax.dot_general(
        left, right, (((1,), (1,)), ((), ())), preferred_element_type=jnp.float32
    )


def contract_first(left, right):
    return lax.dot_general(
        left, right, (((0,), (0,)), ((), ())), preferred_element_type=jnp.float32
    )


def plain_product(left, right):
    return jnp.dot(left, right, preferred_element_type=jnp.float32)


def rope_tables(positions):
    half = HEAD // 2
    freq = THETA ** (-2.0 * jnp.arange(half, dtype=jnp.float32) / HEAD)
    angle = positions.astype(jnp.float32)[:, None] * freq[None, :]
    return (jnp.cos(angle), jnp.sin(angle))


def rotate(value, cosine, sine):
    half = HEAD // 2
    shaped = value.reshape(value.shape[0], -1, HEAD)
    first = shaped[..., :half]
    second = shaped[..., half:]
    cos_rows = cosine[:, None, :]
    sin_rows = sine[:, None, :]
    joined = jnp.concatenate(
        [first * cos_rows - second * sin_rows, second * cos_rows + first * sin_rows], axis=-1
    )
    return joined.reshape(value.shape)


def unrotate(grad, cosine, sine):
    half = HEAD // 2
    shaped = grad.reshape(grad.shape[0], -1, HEAD)
    first = shaped[..., :half]
    second = shaped[..., half:]
    cos_rows = cosine[:, None, :]
    sin_rows = sine[:, None, :]
    joined = jnp.concatenate(
        [first * cos_rows + second * sin_rows, second * cos_rows - first * sin_rows], axis=-1
    )
    return joined.reshape(grad.shape)


def norm_back(value, scale, gain, grad):
    weighted = grad * gain
    inner = jnp.mean(weighted * value, axis=-1, keepdims=True)
    back = scale * weighted - value * (scale * scale * scale) * inner
    return (back, jnp.sum(grad * value * scale, axis=0))


def adamw(weight, gradient, moment, square, rate, decay):
    moment_new = BETA_ONE * moment + (1.0 - BETA_ONE) * gradient
    square_new = BETA_TWO * square + (1.0 - BETA_TWO) * gradient * gradient
    corrected = moment_new / (1.0 - BETA_ONE**STEP)
    spread = jnp.sqrt(square_new / (1.0 - BETA_TWO**STEP)) + ADAM_EPS
    return (weight - rate * (corrected / spread + decay * weight), moment_new, square_new)


AXES = ("dp", "fsdp")
BF16 = jnp.bfloat16
F32 = jnp.float32


def add_low(*values):
    return sum(value.astype(F32) for value in values).astype(BF16)


class Plan:
    def __init__(self, dp, fsdp):
        self.dp, self.fsdp = dp, fsdp
        self.clock = None
        self.bits = [1 << k for k in range(1, (fsdp - 1).bit_length())] + [1]
        self.short = fsdp == 8

    def tie(self, values):
        if self.clock is None:
            return tuple(values)
        return lax.optimization_barrier((tuple(values), self.clock))[0]

    def step(self, work, *values):
        found = work(*self.tie(values))
        self.clock = jax.tree.leaves(found)[0]
        return found

    def window(self, sends, *works):
        values = self.tie([value for value, _ in sends])
        came = []
        for value, (_, mask) in zip(values, sends):
            axis, count = ("fsdp", self.fsdp) if mask > 0 else ("dp", self.dp)
            pairs = [(i, i ^ abs(mask)) for i in range(count)]
            came.append(lax.ppermute(value, axis, pairs))
        gave = [work() for work in works]
        came, self.clock = lax.optimization_barrier((came, self.clock))
        return came, gave

    def wait(self, value):
        value, self.clock = lax.optimization_barrier((value, self.clock))
        return value

    def spread(self, block, marks=None, works=((), (), ())):
        small = marks is not None
        gave = []
        if self.short:
            half = block.shape[0] // 2
            (beside, above, other, *got), found = self.window(
                [(block, 2), (block, 4), (block, 1)] + [(marks, 2)] * small, *works[0]
            )
            gave += found
            if small:
                marks = self.step(lambda a, b: jnp.concatenate([a, b]), marks, *got)
            upper, lower, pair = self.step(
                lambda a, b: (a[:half], b[half:], jnp.concatenate([b, a])), above, beside
            )
            (first, second, pair, *got), found = self.window(
                [(upper, 2), (lower, 4), (pair, 1)] + [(marks, 4)] * small, *works[1]
            )
            gave += found
            across = self.step(lambda a, b: jnp.concatenate([a, b]), first, second)
            if small:
                marks = self.step(lambda a, b: jnp.concatenate([a, b]), marks, *got)
            near = [block, beside, above, across]
            (far, *got), found = self.window(
                [(across, 1)] + [(marks, 1)] * small, *[functools.partial(w, near) for w in works[2]]
            )
            size = block.shape[0]
            return near, [other, pair[:size], pair[size:], far], (marks, *got), gave + found
        near = [block]
        for bit in self.bits[:-1]:
            got, _ = self.window([(piece, bit) for piece in near] + [(marks, bit)] * small)
            if small:
                marks = jnp.concatenate([marks, got[-1]])
            near = near + got[: len(near)]
        for work in [*works[0], *works[1]]:
            gave.append(work())
        got, found = self.window(
            [(piece, 1) for piece in near] + [(marks, 1)] * small,
            *[functools.partial(w, near) for w in works[2]],
        )
        return near, got[: len(near)], (marks, *got[len(near) :]), gave + found

    def settle(self, near, far, rows, works=((), (), ()), small=None):
        gave = []

        def sends(bit):
            return [] if small is None else [(small[bit:], bit)]

        def sum_small(got, bit):
            if got:
                return self.step(lambda a, b: a[:bit] + b, small, *got)
            return None

        if not self.short:
            terms = jnp.concatenate([near(), far])
            for work in [*works[0], *works[1], *works[2]]:
                gave.append(work())
            for bit in reversed(self.bits):
                size = terms.shape[0] // 2
                (got,), _ = self.window([(terms[size:], bit)])
                terms = self.step(add_low, terms[:size], got)
            if small is not None:
                for bit in sorted(self.bits, reverse=True):
                    small = sum_small(self.window(sends(bit))[0], bit)
            return (terms, jnp.zeros_like(terms), jnp.zeros_like(terms)), gave, small
        half = rows // 2
        (got, *more), (near, *found) = self.window([(far, 1)] + sends(4), near, *works[0])
        gave += found
        small = sum_small(more, 4)
        sums = self.step(add_low, near, got)
        across = sums[3 * rows :]
        (first, second, *more), found = self.window(
            [(across[:half], 2), (across[half:], 4)] + sends(2), *works[1]
        )
        gave += found
        small = sum_small(more, 2)

        def merge(sums, first, second):
            beside, above = sums[rows : 2 * rows], sums[2 * rows : 3 * rows]
            return (
                jnp.concatenate([beside[:half], add_low(beside[half:], second)]),
                jnp.concatenate([add_low(above[:half], first), above[half:]]),
            )

        beside, above = self.step(merge, sums, first, second)
        (beside, above, *more), found = self.window([(beside, 2), (above, 4)] + sends(1), *works[2])
        small = sum_small(more, 1)
        return (sums[:rows], beside, above), gave + found, small

    def columns_out(self, shard):
        rows, columns = shard.shape
        width = columns // (self.dp * self.fsdp)
        blocks = shard.reshape(rows, self.dp, self.fsdp, width).transpose(2, 0, 1, 3)
        return lax.all_to_all(
            blocks.reshape(self.fsdp, rows, self.dp * width), "fsdp", 0, 0, tiled=True
        )

    def columns_back(self, blocks):
        rows = blocks.shape[0] // self.fsdp
        width = blocks.shape[1] // self.dp
        blocks = lax.all_to_all(
            blocks.reshape(self.fsdp, rows, self.dp * width), "fsdp", 0, 0, tiled=True
        )
        blocks = blocks.reshape(self.fsdp, rows, self.dp, width).transpose(1, 2, 0, 3)
        return blocks.reshape(rows, self.dp * self.fsdp * width)


def local(
    dp,
    fsdp,
    tokens,
    positions,
    cotangent,
    entry_weight,
    mixing_weight,
    attention_gain,
    expand_weight,
    shrink_weight,
    feedforward_gain,
    entry_moment,
    entry_square,
    mixing_moment,
    mixing_square,
    attention_moment,
    attention_square,
    expand_moment,
    expand_square,
    shrink_moment,
    shrink_square,
    feedforward_moment,
    feedforward_square,
):
    plan = Plan(dp, fsdp)
    step, window, wait = plan.step, plan.window, plan.wait
    rows = tokens.shape[0]
    width = tokens.shape[1]
    group = fsdp // 2
    whole_heads = entry_weight.shape[1] == HEAD
    heads = HEADS // fsdp
    span = heads * HEAD
    factor = HEAD ** (-0.5)
    state = {}

    def work(call, *values):
        return lambda *_: step(call, *values)

    def store(name, call, *values):
        def run(*_):
            state[name] = step(call, *values)

        return run

    def low_of(value):
        return value.astype(BF16)

    join = lambda *a: jnp.concatenate(a)
    product_last = lambda a, b: contract_last(a, b).astype(BF16)
    product_plain = lambda a, b: plain_product(a, b).astype(BF16)

    def product_pairs(a, b, c, d):
        return (contract_first(a, b) + contract_first(c, d)).astype(BF16)

    entry_low = step(low_of, entry_weight)
    role = lax.axis_index("fsdp")
    if whole_heads:
        entry_role = lax.all_gather(entry_low, "dp", axis=1, tiled=True)
    else:
        entry_all = lax.all_gather(entry_low, AXES, axis=1, tiled=True)
        entry_role = lax.dynamic_slice_in_dim(entry_all, role * span, span, axis=1)

    def gains_dp():
        gains = jnp.concatenate([attention_gain, feedforward_gain]).astype(BF16)[:, None]
        return lax.all_gather(gains, "dp", axis=1, tiled=True)

    def gains_fsdp(gains):
        gains = lax.all_gather(gains[:, :, None], "fsdp", axis=2, tiled=True)
        return gains.reshape(2, width).astype(F32)

    def columns_work(shrink_low, mixing_low):
        return plan.columns_out(shrink_low), plan.columns_out(mixing_low)

    def norm_group(gain, places, *blocks):
        group_tokens = jnp.concatenate(blocks)
        group_inputs = group_tokens.astype(F32)
        scale = lax.rsqrt(jnp.mean(group_inputs * group_inputs, axis=-1, keepdims=True) + EPS)
        return (group_inputs * scale * gain).astype(BF16), group_tokens, scale

    def norm_near(near):
        state["near"] = step(norm_group, state["gains"][0], None, *near)

    spread_tokens, far_tokens, (near_places, far_places), _ = plan.spread(
        tokens,
        positions[None],
        (
            [
                store("gate_low", lambda a: a[0].astype(BF16), expand_weight),
                store("gains_dp", gains_dp),
                store("up_low", lambda a: a[1].astype(BF16), expand_weight),
            ],
            [
                lambda: state.update(gains=step(gains_fsdp, state["gains_dp"])),
                store("mixing_low", low_of, mixing_weight[0]),
                store("shrink_low", low_of, shrink_weight[0]),
            ],
            [lambda near: state.update(columns=step(columns_work, state["shrink_low"], state["mixing_low"])), norm_near],
        ),
    )
    gain_one, gain_two = state["gains"][0], state["gains"][1]
    shrink_blocks, mixing_blocks = state["columns"]
    gate_role = lax.all_gather(state["gate_low"], "dp", axis=0, tiled=True)
    if whole_heads:
        mixing_role = lax.all_gather(mixing_blocks, "dp", axis=0, tiled=True).reshape(width, span)
    else:
        mixing_all = lax.all_gather(state["mixing_low"], AXES, axis=0, tiled=True)
        mixing_role = lax.dynamic_slice_in_dim(mixing_all, role * span, span, axis=1)
    up_role = lax.all_gather(state["up_low"], "dp", axis=0, tiled=True)
    shrink_role = lax.all_gather(shrink_blocks, "dp", axis=0, tiled=True).reshape(width, -1)

    def heads_of(value):
        return value.reshape(group, rows, heads, HEAD)

    def project(normed, entry_role, places):
        cosine, sine = rope_tables(places.reshape(-1))
        mixed = contract_last(normed, entry_role)
        return (
            rotate(mixed[:, :span], cosine, sine).astype(BF16),
            rotate(mixed[:, span : 2 * span], cosine, sine).astype(BF16),
            mixed[:, 2 * span :].astype(BF16),
            cosine,
            sine,
        )

    def attend(query, keys, values, places):
        slots = jnp.arange(rows, dtype=jnp.int32)
        same = places[:, :, None] - places[:, None, :] == slots[:, None] - slots[None, :]
        visible = (same & (slots[None, :] <= slots[:, None]))[:, None]
        raw = jnp.einsum(
            "bqhd,bkhd->bhqk", heads_of(query), heads_of(keys), preferred_element_type=F32
        )
        scores = jnp.where(visible, raw * factor, -1e30)
        top = jnp.max(scores, axis=-1, keepdims=True)
        weights = jnp.exp(scores - top)
        probs_full = weights / jnp.sum(weights, axis=-1, keepdims=True)
        attended = (
            jnp.einsum(
                "bhqk,bkhd->bqhd",
                probs_full.astype(BF16),
                heads_of(values),
                preferred_element_type=F32,
            )
            .reshape(group * rows, span)
            .astype(BF16)
        )
        return attended, probs_full

    inputs = tokens.astype(F32)
    live = (positions >= 0).astype(F32)[:, None]
    grad_out = cotangent.astype(F32) * live
    grad_low = step(low_of, grad_out)
    state["far"] = step(norm_group, gain_one, None, *far_tokens)
    entry_role = wait(entry_role).reshape(3 * span, width)

    def project_work(name, places):
        def run(*_):
            state["qkv " + name] = step(project, state[name][0], entry_role, places)

        return run

    def attend_work(name, places):
        def run(*_):
            state["attend " + name] = step(attend, *state["qkv " + name][:3], places)

        return run

    near_grad, far_grad, _, _ = plan.spread(
        grad_low,
        None,
        (
            [project_work("far", far_places), project_work("near", near_places)],
            [attend_work("far", far_places)],
            [attend_work("near", near_places)],
        ),
    )
    gate_role = wait(gate_role)
    mixing_role = wait(mixing_role)
    far = step(product_last, state["attend far"][0], mixing_role)
    near = work(product_last, state["attend near"][0], mixing_role)
    parts, _, _ = plan.settle(
        near, far, rows, ([], [store("grad near", join, *near_grad)], [store("grad far", join, *far_grad)])
    )

    def norm_middle(inputs, gain, own, beside, above):
        middle = inputs + own.astype(F32) + beside.astype(F32) + above.astype(F32)
        scale = lax.rsqrt(jnp.mean(middle * middle, axis=-1, keepdims=True) + EPS)
        return (middle * scale * gain).astype(BF16), middle, scale

    low_two, middle, scale_two = step(norm_middle, inputs, gain_two, *parts)

    def expand(normed, gate_role, up_role):
        gate = contract_last(normed, gate_role)
        upward = contract_last(normed, up_role)
        return gate, upward, (gate * jax.nn.sigmoid(gate) * upward).astype(BF16)

    def expand_near(near):
        state["two near"] = step(join, *near)
        state["up near"] = step(expand, state["two near"], gate_role, wait(up_role))

    _, far_two, _, _ = plan.spread(low_two, None, ([], [], [expand_near]))
    state["two far"] = step(join, *far_two)
    state["up far"] = step(expand, state["two far"], gate_role, up_role)
    shrink_grad = step(
        product_pairs, state["grad near"], state["up near"][2], state["grad far"], state["up far"][2]
    )
    shrink_summed = lax.psum_scatter(shrink_grad, "dp", scatter_dimension=0, tiled=True)
    shrink_role = wait(shrink_role)

    def back(gate, upward, grad_group, shrink_role):
        sigma = jax.nn.sigmoid(gate)
        swish = gate * sigma
        hidden_grad = plain_product(grad_group, shrink_role)
        gate_grad = hidden_grad * upward * (sigma * (1.0 + gate * (1.0 - sigma)))
        upward_grad = hidden_grad * swish
        return gate_grad.astype(BF16), upward_grad.astype(BF16)

    def back_terms(gate_grad, up_grad, gate_role, up_role):
        return (plain_product(gate_grad, gate_role) + plain_product(up_grad, up_role)).astype(BF16)

    far_back = step(back, *state["up far"][:2], state["grad far"], shrink_role)
    far = step(back_terms, *far_back, gate_role, up_role)
    near_back = step(back, *state["up near"][:2], state["grad near"], shrink_role)

    def expand_grad(index):
        return work(
            product_pairs, near_back[index], state["two near"], far_back[index], state["two far"]
        )

    parts, (gate_grad, up_grad), _ = plan.settle(
        work(back_terms, *near_back, gate_role, up_role),
        far,
        rows,
        ([], [expand_grad(0)], [expand_grad(1)]),
    )
    gate_summed = lax.psum_scatter(gate_grad, "dp", scatter_dimension=0, tiled=True)
    up_summed = lax.psum_scatter(up_grad, "dp", scatter_dimension=0, tiled=True)

    shrink_summed = wait(shrink_summed)

    def shrink_update(summed, *values):
        gradient = plan.columns_back(summed)[None].astype(F32)
        return gradient, *adamw(values[0], gradient, *values[1:], RATE, DECAY)

    def expand_update(gate, up, weight, moment, square):
        gradient = jnp.stack([gate, up]).astype(F32)
        return gradient, *adamw(weight, gradient, moment, square, RATE, DECAY)

    def back_two(middle, scale, gain, grad_out, own, beside, above):
        grad = own.astype(F32) + beside.astype(F32) + above.astype(F32)
        middle_back, gain_grad = norm_back(middle, scale, gain, grad)
        middle_grad = grad_out + middle_back
        return middle_grad.astype(BF16), middle_grad, gain_grad

    branch_low, middle_grad, gain_two_grad = step(
        back_two, middle, scale_two, gain_two, grad_out, *parts
    )

    def branch_near(near):
        state["branch near"] = step(join, *near)
        state["do near"] = step(product_plain, state["branch near"], mixing_role)

    _, far_branch, _, (far_output, near_output, *_) = plan.spread(
        branch_low,
        None,
        (
            [
                work(product_last, state["up far"][2], shrink_role),
                work(product_last, state["up near"][2], shrink_role),
            ],
            [store("shrink", shrink_update, shrink_summed, shrink_weight, shrink_moment, shrink_square)],
            [branch_near],
        ),
    )
    state["branch far"] = step(join, *far_branch)
    state["do far"] = step(product_plain, state["branch far"], mixing_role)

    gate_summed = wait(gate_summed)

    def attend_back(query, keys, values, cosine, sine, probs_full, attended_grad):
        query_heads, key_heads, value_heads = heads_of(query), heads_of(keys), heads_of(values)
        attended_grad = heads_of(attended_grad)
        prob_grad = jnp.einsum(
            "bqhd,bkhd->bhqk", attended_grad, value_heads, preferred_element_type=F32
        )
        delta = jnp.sum(probs_full * prob_grad, axis=-1, keepdims=True)
        score_grad = (probs_full * (prob_grad - delta)).astype(BF16)
        value_grad = jnp.einsum(
            "bhqk,bqhd->bkhd", probs_full.astype(BF16), attended_grad, preferred_element_type=F32
        ).reshape(group * rows, span)
        query_grad = (
            jnp.einsum(
                "bhqk,bkhd->bqhd", score_grad, key_heads, preferred_element_type=F32
            ).reshape(group * rows, span)
            * factor
        )
        key_grad = (
            jnp.einsum(
                "bhqk,bqhd->bkhd", score_grad, query_heads, preferred_element_type=F32
            ).reshape(group * rows, span)
            * factor
        )
        return jnp.concatenate(
            [unrotate(query_grad, cosine, sine), unrotate(key_grad, cosine, sine), value_grad],
            axis=1,
        ).astype(BF16)

    def attend_back_work(name):
        return store(
            "mixed " + name,
            attend_back,
            *state["qkv " + name],
            state["attend " + name][1],
            state["do " + name],
        )

    parts, (mixing_grad, *_), _ = plan.settle(
        lambda: near_output,
        far_output,
        rows,
        (
            [
                work(
                    product_pairs,
                    state["branch near"],
                    state["attend near"][0],
                    state["branch far"],
                    state["attend far"][0],
                )
            ],
            [attend_back_work("far")],
            [attend_back_work("near")],
        ),
    )
    if whole_heads:
        mixing_summed = lax.psum_scatter(mixing_grad, "dp", scatter_dimension=0, tiled=True)
    layer_output = step(
        lambda *a: sum((value.astype(F32) for value in a[1:]), a[0]).astype(BF16), middle, *parts
    )
    up_summed = wait(up_summed)

    def back_one(mixed_grad, entry_role, group_tokens, scale):
        part = plain_product(mixed_grad, entry_role)
        gain_grad = jnp.sum(part * group_tokens.astype(F32) * scale, axis=0)
        return part.astype(BF16), gain_grad

    far, far_gain = step(back_one, state["mixed far"], entry_role, *state["far"][1:])
    near, near_gain = step(back_one, state["mixed near"], entry_role, *state["near"][1:])

    def order_gains(far_gain, near_gain, gain_two_grad):
        gains = jnp.stack([far_gain + near_gain, gain_two_grad])
        gains = gains.reshape(2, dp, fsdp, width // (dp * fsdp)).transpose(2, 1, 0, 3)
        return jnp.take(gains, jnp.arange(fsdp) ^ role, axis=0)

    gains = step(order_gains, far_gain, near_gain, gain_two_grad)
    parts, (entry_grad, *_), gains = plan.settle(
        lambda: near,
        far,
        rows,
        (
            [
                work(
                    product_pairs,
                    state["mixed near"],
                    state["near"][0],
                    state["mixed far"],
                    state["far"][0],
                )
            ],
            [],
            [
                store(
                    "expand",
                    expand_update,
                    gate_summed,
                    up_summed,
                    expand_weight,
                    expand_moment,
                    expand_square,
                )
            ],
        ),
        gains,
    )
    shrink_gradient, *shrink_new = state["shrink"]
    expand_gradient, *expand_new = state["expand"]
    if whole_heads:
        entry_gradient = lax.psum_scatter(
            entry_grad.reshape(3, dp * HEAD, width), "dp", scatter_dimension=1, tiled=True
        )
    else:
        entry_full = lax.dynamic_update_slice_in_dim(
            jnp.zeros((3, width, width), BF16),
            entry_grad.reshape(3, span, width),
            role * span,
            axis=1,
        )
        mixing_full = lax.dynamic_update_slice_in_dim(
            jnp.zeros((width, width), BF16), mixing_grad, role * span, axis=1
        )
        entry_gradient = lax.psum_scatter(entry_full, AXES, scatter_dimension=1, tiled=True)
        mixing_gradient = lax.psum_scatter(mixing_full, AXES, scatter_dimension=0, tiled=True)

    def back_input(inputs, gain, middle_grad, *parts):
        scale = lax.rsqrt(jnp.mean(inputs * inputs, axis=-1, keepdims=True) + EPS)
        grad = sum(value.astype(F32) for value in parts)
        return middle_grad + norm_back(inputs, scale, gain, grad)[0]

    input_gradient = step(back_input, inputs, gain_one, middle_grad, *parts)

    def order_dp(gains):
        return jnp.take(gains[0], jnp.arange(dp) ^ lax.axis_index("dp"), axis=0)

    gains = step(order_dp, gains)
    for bit in reversed([1 << k for k in range((dp - 1).bit_length())]):
        (got,), _ = window([(gains[bit:], -bit)])
        gains = step(lambda a, b: a[:bit] + b, gains, got)
    gain_grads = gains[0]
    attention_gradient, feedforward_gradient = gain_grads[:1], gain_grads[1:]

    if whole_heads:
        mixing_gradient = step(plan.columns_back, mixing_summed)
    mixing_gradient = mixing_gradient[None].astype(F32)
    entry_gradient = entry_gradient.astype(F32)
    entry_new = adamw(entry_weight, entry_gradient, entry_moment, entry_square, RATE, DECAY)
    mixing_new = adamw(
        mixing_weight, mixing_gradient, mixing_moment, mixing_square, MIXING_RATE, DECAY
    )
    attention_new = adamw(
        attention_gain, attention_gradient, attention_moment, attention_square, GAIN_RATE, 0.0
    )
    feedforward_new = adamw(
        feedforward_gain,
        feedforward_gradient,
        feedforward_moment,
        feedforward_square,
        GAIN_RATE,
        0.0,
    )
    return (
        layer_output,
        input_gradient,
        entry_gradient,
        mixing_gradient,
        attention_gradient,
        expand_gradient,
        shrink_gradient,
        feedforward_gradient,
        entry_new[0],
        mixing_new[0],
        attention_new[0],
        expand_new[0],
        shrink_new[0],
        feedforward_new[0],
        entry_new[1],
        entry_new[2],
        mixing_new[1],
        mixing_new[2],
        attention_new[1],
        attention_new[2],
        expand_new[1],
        expand_new[2],
        shrink_new[1],
        shrink_new[2],
        feedforward_new[1],
        feedforward_new[2],
    )


def solution(mesh):
    placed = (
        P(("dp", "fsdp"), None),
        P(("dp", "fsdp")),
        P(("dp", "fsdp"), None),
        P(None, ("dp", "fsdp"), None),
        P(None, ("dp", "fsdp"), None),
        P(None, ("dp", "fsdp")),
        P(None, ("dp", "fsdp"), None),
        P(None, ("dp", "fsdp"), None),
        P(None, ("dp", "fsdp")),
        P(None, ("dp", "fsdp"), None),
        P(None, ("dp", "fsdp"), None),
        P(None, ("dp", "fsdp"), None),
        P(None, ("dp", "fsdp"), None),
        P(None, ("dp", "fsdp")),
        P(None, ("dp", "fsdp")),
        P(None, ("dp", "fsdp"), None),
        P(None, ("dp", "fsdp"), None),
        P(None, ("dp", "fsdp"), None),
        P(None, ("dp", "fsdp"), None),
        P(None, ("dp", "fsdp")),
        P(None, ("dp", "fsdp")),
    )
    return jax.shard_map(
        functools.partial(local, mesh.shape["dp"], mesh.shape["fsdp"]),
        mesh=mesh,
        in_specs=placed,
        out_specs=(
            P(("dp", "fsdp"), None),
            P(("dp", "fsdp"), None),
            P(None, ("dp", "fsdp"), None),
            P(None, ("dp", "fsdp"), None),
            P(None, ("dp", "fsdp")),
            P(None, ("dp", "fsdp"), None),
            P(None, ("dp", "fsdp"), None),
            P(None, ("dp", "fsdp")),
            P(None, ("dp", "fsdp"), None),
            P(None, ("dp", "fsdp"), None),
            P(None, ("dp", "fsdp")),
            P(None, ("dp", "fsdp"), None),
            P(None, ("dp", "fsdp"), None),
            P(None, ("dp", "fsdp")),
            P(None, ("dp", "fsdp"), None),
            P(None, ("dp", "fsdp"), None),
            P(None, ("dp", "fsdp"), None),
            P(None, ("dp", "fsdp"), None),
            P(None, ("dp", "fsdp")),
            P(None, ("dp", "fsdp")),
            P(None, ("dp", "fsdp"), None),
            P(None, ("dp", "fsdp"), None),
            P(None, ("dp", "fsdp"), None),
            P(None, ("dp", "fsdp"), None),
            P(None, ("dp", "fsdp")),
            P(None, ("dp", "fsdp")),
        ),
        check_vma=False,
    )
```

```python
import functools

import jax
import jax.numpy as jnp
from jax import lax
from jax.experimental import pallas as pl
from jax.experimental.pallas import tpu as pltpu
from jax.sharding import PartitionSpec as P

HEADS = 32
HEAD = 64
STEP = 3


EPS = 1e-05
THETA = 130000.0
RATE = 0.01
MIXING_RATE = 0.04
GAIN_RATE = 0.3
BETA_ONE = 0.9
BETA_TWO = 0.95
ADAM_EPS = 1e-08
DECAY = 0.1


def contract_last(left, right):
    return lax.dot_general(
        left, right, (((1,), (1,)), ((), ())), preferred_element_type=jnp.float32
    )


def contract_first(left, right):
    return lax.dot_general(
        left, right, (((0,), (0,)), ((), ())), preferred_element_type=jnp.float32
    )


def plain_product(left, right):
    return jnp.dot(left, right, preferred_element_type=jnp.float32)


def rope_tables(positions):
    half = HEAD // 2
    freq = THETA ** (-2.0 * jnp.arange(half, dtype=jnp.float32) / HEAD)
    angle = positions.astype(jnp.float32)[:, None] * freq[None, :]
    return (jnp.cos(angle), jnp.sin(angle))


def norm_back(value, scale, gain, grad):
    weighted = grad * gain
    inner = jnp.mean(weighted * value, axis=-1, keepdims=True)
    back = scale * weighted - value * (scale * scale * scale) * inner
    return (back, jnp.sum(grad * value * scale, axis=0))


def adamw(weight, gradient, moment, square, rate, decay):
    moment_new = BETA_ONE * moment + (1.0 - BETA_ONE) * gradient
    square_new = BETA_TWO * square + (1.0 - BETA_TWO) * gradient * gradient
    corrected = moment_new / (1.0 - BETA_ONE**STEP)
    spread = jnp.sqrt(square_new / (1.0 - BETA_TWO**STEP)) + ADAM_EPS
    return (weight - rate * (corrected / spread + decay * weight), moment_new, square_new)


AXES = ("dp", "fsdp")
VMEM_BYTES = 56 * 2**20
BF16 = jnp.bfloat16
F32 = jnp.float32


def add_low(*values):
    return sum(value.astype(F32) for value in values).astype(BF16)


def probs_of(left, right, places_down, places_across, turned):
    rows = right.shape[0]
    down = lax.broadcasted_iota(jnp.int32, (rows, rows), 0)
    across = lax.broadcasted_iota(jnp.int32, (rows, rows), 1)
    earlier = down <= across if turned else across <= down
    visible = (places_down - places_across == down - across) & earlier
    raw = contract_last(left, right).reshape(-1, rows, rows)
    scores = jnp.where(visible[None], raw * (HEAD ** (-0.5)), -1e30)
    axis = 1 if turned else 2
    weights = jnp.exp(scores - jnp.max(scores, axis=axis, keepdims=True))
    return weights * (1.0 / jnp.sum(weights, axis=axis, keepdims=True))


def by_head(value):
    head = lax.broadcasted_iota(jnp.int32, value.shape, 1) // HEAD
    none = jnp.zeros_like(value)
    return jnp.concatenate(
        [jnp.where(head == h, value, none) for h in range(value.shape[1] // HEAD)]
    )


def own_columns(value, rows):
    head = lax.broadcasted_iota(jnp.int32, (rows, value.shape[1]), 1) // HEAD
    total = value[:rows]
    for h in range(1, value.shape[1] // HEAD):
        total = jnp.where(head == h, value[h * rows : (h + 1) * rows], total)
    return total


def swap_halves(value):
    columns = value.shape[1]
    half = HEAD // 2
    lane = lax.broadcasted_iota(jnp.int32, value.shape, 1) % HEAD
    return jnp.where(
        lane < half, pltpu.roll(value, columns - half, 1), pltpu.roll(value, half, 1)
    )


def attend_kernel(group, *refs):
    blocks, refs = refs[:group], refs[group:]
    gain, weight, cosine, sine, down, across, normed, joint, attended, held = refs
    for k in range(group):

        @pl.when(pl.program_id(0) == k)
        def _():
            held[...] = blocks[k][...]

    value = held[...].astype(F32)
    scale = lax.rsqrt(jnp.mean(value * value, axis=-1, keepdims=True) + EPS)
    normed[...] = (value * scale * gain[...]).astype(BF16)
    mixed = contract_last(normed[...], weight[...])
    span = mixed.shape[1] // 3
    for part in range(2):
        piece = mixed[:, part * span : (part + 1) * span]
        joint[:, part * span : (part + 1) * span] = (
            piece * cosine[...] + swap_halves(piece) * sine[...]
        ).astype(BF16)
    joint[:, 2 * span :] = mixed[:, 2 * span :].astype(BF16)
    query, keys, values = (joint[:, part * span : (part + 1) * span] for part in range(3))
    rows = query.shape[0]
    probs = probs_of(by_head(query), keys, down[0], across[0], False).astype(BF16)
    found = plain_product(probs.reshape(-1, rows), values)
    attended[...] = own_columns(found, rows).astype(BF16)


def attend_blocks(blocks, gain, weight, cosine, sine, places):
    group = len(blocks)
    rows, width = blocks[0].shape
    span = weight.shape[0] // 3
    whole = lambda *shape: pl.BlockSpec(shape, lambda i: (0,) * len(shape))
    by_row = lambda columns: pl.BlockSpec((rows, columns), lambda i: (i, 0))
    return pl.pallas_call(
        functools.partial(attend_kernel, group),
        grid=(group,),
        in_specs=[whole(rows, width)] * group
        + [whole(1, width), whole(3 * span, width), by_row(span), by_row(span)]
        + [
            pl.BlockSpec((1, rows, 1), lambda i: (i, 0, 0)),
            pl.BlockSpec((1, 1, rows), lambda i: (i, 0, 0)),
        ],
        out_specs=[by_row(width), by_row(3 * span), by_row(span)],
        out_shape=[
            jax.ShapeDtypeStruct((group * rows, columns), BF16)
            for columns in (width, 3 * span, span)
        ],
        scratch_shapes=[pltpu.VMEM((rows, width), BF16)],
        compiler_params=pltpu.CompilerParams(vmem_limit_bytes=VMEM_BYTES),
    )(*blocks, gain[None], weight, cosine, sine, places[:, :, None], places[:, None, :])


def attend_back_kernel(group, first, *refs):
    grads, blocks, refs = refs[:group], refs[group : 2 * group], refs[2 * group :]
    mixing, weight, joint, attended, normed, cosine, sine, down, across = refs[:9]
    earlier, refs = (None, refs[9:]) if first else (refs[9:12], refs[12:])
    terms, entry_sum, mixing_sum, gain_sum, held, tokens, back = refs
    step = pl.program_id(0)
    for k in range(group):

        @pl.when(step == k)
        def _():
            held[...] = grads[k][...]
            tokens[...] = blocks[k][...]

    @pl.when(step == 0)
    def _():
        for k, sums in ((1, mixing_sum), (2, gain_sum)):
            sums[...] = jnp.zeros_like(sums) if first else earlier[k][...]

    rows = held.shape[0]
    here = pl.ds(pl.multiple_of(step * rows, rows), rows)
    span = joint.shape[1] // 3
    query, keys, values = (joint[:, part * span : (part + 1) * span] for part in range(3))
    grad = plain_product(held[...], mixing[...]).astype(BF16)
    key_heads = by_head(keys)
    probs = probs_of(key_heads, query, down[0], across[0], True)
    prob_grad = contract_last(by_head(values), grad).reshape(probs.shape)
    delta = jnp.sum(probs * prob_grad, axis=1, keepdims=True)
    score_grad = (probs * (prob_grad - delta)).astype(BF16).reshape(-1, rows)
    query_grad = contract_first(score_grad, key_heads)
    key_grad = own_columns(plain_product(score_grad, query), rows)
    value_grad = own_columns(plain_product(probs.astype(BF16).reshape(-1, rows), grad), rows)
    for part, value in enumerate((query_grad, key_grad)):
        value = value * (HEAD ** (-0.5))
        back[here, part * span : (part + 1) * span] = (
            value * cosine[...] - swap_halves(value) * sine[...]
        ).astype(BF16)
    back[here, 2 * span :] = value_grad.astype(BF16)
    term = plain_product(back[here, :], weight[...])
    terms[...] = term.astype(BF16)
    value = tokens[...].astype(F32)
    scale = lax.rsqrt(jnp.mean(value * value, axis=-1, keepdims=True) + EPS)
    gain_sum[...] += jnp.sum(term * (value * scale), axis=0, keepdims=True)
    mixing_sum[...] += contract_first(attended[...], held[...])

    @pl.when(step == group - 1)
    def _():
        for part in range(3):
            part = slice(part * span, (part + 1) * span)
            found = contract_first(back[:, part], normed[...])
            entry_sum[part, :] = found if first else earlier[0][part, :] + found


def attend_back_blocks(grads, blocks, mixing, weight, joint, attended, normed, turn, places, earlier):
    group = len(blocks)
    rows, width = blocks[0].shape
    span = weight.shape[0] // 3
    whole = lambda *shape: pl.BlockSpec(shape, lambda i: (0,) * len(shape))
    by_row = lambda columns: pl.BlockSpec((rows, columns), lambda i: (i, 0))
    sums = [(3 * span, width), (span, width), (1, width)]
    return pl.pallas_call(
        functools.partial(attend_back_kernel, group, not earlier),
        grid=(group,),
        in_specs=[whole(rows, width)] * (2 * group)
        + [whole(width, span), whole(3 * span, width)]
        + [by_row(3 * span), by_row(span), whole(group * rows, width), by_row(span), by_row(span)]
        + [
            pl.BlockSpec((1, rows, 1), lambda i: (i, 0, 0)),
            pl.BlockSpec((1, 1, rows), lambda i: (i, 0, 0)),
        ]
        + [whole(*shape) for shape in sums if earlier],
        out_specs=[by_row(width)] + [whole(*shape) for shape in sums],
        out_shape=[jax.ShapeDtypeStruct((group * rows, width), BF16)]
        + [jax.ShapeDtypeStruct(shape, F32) for shape in sums],
        scratch_shapes=[
            pltpu.VMEM((rows, width), BF16),
            pltpu.VMEM((rows, width), BF16),
            pltpu.VMEM((group * rows, 3 * span), BF16),
        ],
        compiler_params=pltpu.CompilerParams(vmem_limit_bytes=VMEM_BYTES),
    )(
        *grads,
        *blocks,
        mixing,
        weight,
        joint,
        attended,
        normed,
        *turn,
        places[:, :, None],
        places[:, None, :],
        *earlier,
    )


def turn_tables(places, heads):
    cosine, sine = rope_tables(places.reshape(-1))
    return (
        jnp.tile(jnp.concatenate([cosine, cosine], axis=1), (1, heads)),
        jnp.tile(jnp.concatenate([-sine, sine], axis=1), (1, heads)),
    )


class Plan:
    def __init__(self, dp, fsdp):
        self.dp, self.fsdp = dp, fsdp
        self.clock = None
        self.bits = [1 << k for k in range(1, (fsdp - 1).bit_length())] + [1]
        self.short = fsdp == 8

    def tie(self, values):
        if self.clock is None:
            return tuple(values)
        return lax.optimization_barrier((tuple(values), self.clock))[0]

    def step(self, work, *values):
        found = work(*self.tie(values))
        self.clock = jax.tree.leaves(found)
        return found

    def window(self, sends, *works):
        values = self.tie([value for value, _ in sends])
        came = []
        for value, (_, mask) in zip(values, sends):
            axis, count = ("fsdp", self.fsdp) if mask > 0 else ("dp", self.dp)
            pairs = [(i, i ^ abs(mask)) for i in range(count)]
            came.append(lax.ppermute(value, axis, pairs))
        gave, done = [], []
        for work in works:
            gave.append(work())
            done += self.clock
        came, self.clock = lax.optimization_barrier((came, done or came))
        return came, gave

    def wait(self, value):
        self.clock = [*self.clock, value]
        return value

    def merge(self, rows, sums, first, second):
        half = rows // 2
        beside, above = sums[rows : 2 * rows], sums[2 * rows : 3 * rows]
        return (
            jnp.concatenate([beside[:half], add_low(beside[half:], second)]),
            jnp.concatenate([add_low(above[:half], first), above[half:]]),
        )

    def spread(self, block, marks=None, works=((), (), ()), extra=None):
        small = marks is not None
        gave, more = [], []

        def added(k):
            return [] if extra is None else extra(k, more)

        if self.short:
            half = block.shape[0] // 2
            (beside, above, other, *got), found = self.window(
                [(block, 2), (block, 4), (block, 1)] + [(marks, 2)] * small + added(0), *works[0]
            )
            gave += found
            more.append(got)
            if small:
                marks = self.step(lambda a, b: jnp.concatenate([a, b]), marks, *got)
            upper, lower, pair = self.step(
                lambda a, b: (a[:half], b[half:], jnp.concatenate([b, a])), above, beside
            )
            (first, second, pair, *got), found = self.window(
                [(upper, 2), (lower, 4), (pair, 1)] + [(marks, 4)] * small, *works[1]
            )
            gave += found
            across = self.step(lambda a, b: jnp.concatenate([a, b]), first, second)
            if small:
                marks = self.step(lambda a, b: jnp.concatenate([a, b]), marks, *got)
            near = [block, beside, above, across]
            (far, *got), found = self.window(
                [(across, 1)] + [(marks, 1)] * small + added(2),
                *[functools.partial(w, near) for w in works[2]],
            )
            more.append(got)
            size = block.shape[0]
            got = got if extra is None else more
            return near, [other, pair[:size], pair[size:], far], (marks, *got), gave + found
        near = [block]
        for bit in self.bits[:-1]:
            got, _ = self.window([(piece, bit) for piece in near] + [(marks, bit)] * small)
            if small:
                marks = jnp.concatenate([marks, got[-1]])
            near = near + got[: len(near)]
        for work in [*works[0], *works[1]]:
            gave.append(work())
        got, found = self.window(
            [(piece, 1) for piece in near] + [(marks, 1)] * small,
            *[functools.partial(w, near) for w in works[2]],
        )
        return near, got[: len(near)], (marks, *got[len(near) :]), gave + found

    def settle(self, near, far, rows, works=((), (), ()), small=None, got=None):
        gave = []

        def sends(bit):
            return [] if small is None else [(small[bit:], bit)]

        def sum_small(got, bit):
            if got:
                return self.step(lambda a, b: a[:bit] + b, small, *got)
            return None

        if not self.short:
            terms = jnp.concatenate([near(), far])
            for work in [*works[0], *works[1], *works[2]]:
                gave.append(work())
            for bit in reversed(self.bits):
                size = terms.shape[0] // 2
                if got is None:
                    (got,), _ = self.window([(terms[size:], bit)])
                terms = self.step(add_low, terms[:size], got)
                got = None
            if small is not None:
                for bit in sorted(self.bits, reverse=True):
                    small = sum_small(self.window(sends(bit))[0], bit)
            return (terms, jnp.zeros_like(terms), jnp.zeros_like(terms)), gave, small
        half = rows // 2
        if got is None:
            (got,), (near, *found) = self.window([(far, 1)], near, *works[0])
            gave += found
        else:
            near = near()
        sums = self.step(add_low, near, got)
        across = sums[3 * rows :]
        (first, second, *more), found = self.window(
            [(across[:half], 2), (across[half:], 4)] + sends(4), *works[1]
        )
        gave += found
        small = sum_small(more, 4)

        beside, above = self.step(functools.partial(self.merge, rows), sums, first, second)
        (beside, above, *more), found = self.window([(beside, 2), (above, 4)] + sends(2), *works[2])
        small = sum_small(more, 2)
        if small is not None:
            (more,), _ = self.window(sends(1))
            small = sum_small([more], 1)
        return (sums[:rows], beside, above), gave + found, small

    def columns_split(self, shard):
        rows, columns = shard.shape
        width = columns // (self.dp * self.fsdp)
        blocks = shard.reshape(rows, self.dp, self.fsdp, width).transpose(2, 0, 1, 3)
        return blocks.reshape(self.fsdp, rows, self.dp * width)

    def exchange(self, blocks):
        return lax.all_to_all(blocks, "fsdp", 0, 0, tiled=True)

    def columns_back(self, blocks):
        rows = blocks.shape[0] // self.fsdp
        width = blocks.shape[1] // self.dp
        blocks = lax.all_to_all(
            blocks.reshape(self.fsdp, rows, self.dp * width), "fsdp", 0, 0, tiled=True
        )
        blocks = blocks.reshape(self.fsdp, rows, self.dp, width).transpose(1, 2, 0, 3)
        return blocks.reshape(rows, self.dp * self.fsdp * width)


def local(
    dp,
    fsdp,
    tokens,
    positions,
    cotangent,
    entry_weight,
    mixing_weight,
    attention_gain,
    expand_weight,
    shrink_weight,
    feedforward_gain,
    entry_moment,
    entry_square,
    mixing_moment,
    mixing_square,
    attention_moment,
    attention_square,
    expand_moment,
    expand_square,
    shrink_moment,
    shrink_square,
    feedforward_moment,
    feedforward_square,
):
    plan = Plan(dp, fsdp)
    step, window, wait = plan.step, plan.window, plan.wait
    rows = tokens.shape[0]
    width = tokens.shape[1]
    group = fsdp // 2
    whole_heads = entry_weight.shape[1] == HEAD
    heads = HEADS // fsdp
    span = heads * HEAD
    factor = HEAD ** (-0.5)
    state = {}

    def work(call, *values):
        return lambda *_: step(call, *values)

    def store(name, call, *values):
        def run(*_):
            state[name] = step(call, *values)

        return run

    def low_of(value):
        return value.astype(BF16)

    join = lambda *a: jnp.concatenate(a)
    product_last = lambda a, b: contract_last(a, b).astype(BF16)
    product_plain = lambda a, b: plain_product(a, b).astype(BF16)

    def product_pairs(a, b, c, d):
        return (contract_first(a, b) + contract_first(c, d)).astype(BF16)

    entry_low = step(low_of, entry_weight)
    role = lax.axis_index("fsdp")
    if whole_heads:
        entry_role = lax.all_gather(entry_low, "dp", axis=1, tiled=True)
    else:
        entry_all = lax.all_gather(entry_low, AXES, axis=1, tiled=True)
        entry_role = lax.dynamic_slice_in_dim(entry_all, role * span, span, axis=1)

    def gains_dp(*gains):
        gains = jnp.concatenate(gains).astype(BF16)[:, None]
        return lax.all_gather(gains, "dp", axis=1, tiled=True)

    def gains_fsdp(gains):
        gains = lax.all_gather(gains[:, :, None], "fsdp", axis=2, tiled=True)
        return gains.reshape(2, width).astype(F32)

    def columns_work(shrink_low, mixing_low):
        blocks = plan.exchange(
            jnp.concatenate([plan.columns_split(shrink_low), plan.columns_split(mixing_low)], -1)
        )
        size = shrink_low.shape[1] // fsdp
        return blocks[..., :size], blocks[..., size:]

    spread_tokens, far_tokens, (near_places, far_places), _ = plan.spread(
        tokens,
        positions[None],
        (
            [
                store("mixing_low", low_of, mixing_weight[0]),
                store("shrink_low", low_of, shrink_weight[0]),
                store("gains_dp", gains_dp, attention_gain, feedforward_gain),
                lambda: state.update(
                    columns=step(columns_work, state["shrink_low"], state["mixing_low"])
                ),
            ],
            [
                store("gate_low", lambda a: a[0].astype(BF16), expand_weight),
                store("up_low", lambda a: a[1].astype(BF16), expand_weight),
                lambda: state.update(gains=step(gains_fsdp, state["gains_dp"])),
            ],
            [],
        ),
    )
    gain_one, gain_two = state["gains"][0], state["gains"][1]
    shrink_blocks, mixing_blocks = state["columns"]
    gate_role = lax.all_gather(state["gate_low"], "dp", axis=0, tiled=True)
    if whole_heads:
        mixing_role = lax.all_gather(mixing_blocks, "dp", axis=0, tiled=True).reshape(width, span)
    else:
        mixing_all = lax.all_gather(state["mixing_low"], AXES, axis=0, tiled=True)
        mixing_role = lax.dynamic_slice_in_dim(mixing_all, role * span, span, axis=1)
    up_role = lax.all_gather(state["up_low"], "dp", axis=0, tiled=True)
    shrink_role = lax.all_gather(shrink_blocks, "dp", axis=0, tiled=True).reshape(width, -1)

    inputs = tokens.astype(F32)
    live = (positions >= 0).astype(F32)[:, None]
    grad_out = cotangent.astype(F32) * live
    grad_low = step(low_of, grad_out)
    entry_role = wait(entry_role).reshape(3 * span, width)
    state["turn near"] = step(lambda a: turn_tables(a, heads), near_places)
    state["turn far"] = step(lambda a: turn_tables(a, heads), far_places)

    def attend_work(name, blocks, places):
        def run(*_):
            state["attend " + name] = step(
                attend_blocks, blocks, gain_one, entry_role, *state["turn " + name], places
            )

        return run

    near_grad, far_grad, _, _ = plan.spread(
        grad_low,
        None,
        (
            [attend_work("far", far_tokens, far_places)],
            [
                attend_work("near", spread_tokens, near_places),
                lambda: state.update(gate=wait(gate_role)),
            ],
            [],
        ),
    )
    mixing_role = wait(mixing_role)
    far = step(product_last, state["attend far"][2], mixing_role)
    near = work(product_last, state["attend near"][2], mixing_role)
    parts, _, _ = plan.settle(
        near, far, rows, ([], [store("grad near", join, *near_grad)], [store("grad far", join, *far_grad)])
    )

    def norm_middle(inputs, gain, own, beside, above):
        middle = inputs + own.astype(F32) + beside.astype(F32) + above.astype(F32)
        scale = lax.rsqrt(jnp.mean(middle * middle, axis=-1, keepdims=True) + EPS)
        return (middle * scale * gain).astype(BF16), middle, scale

    low_two, middle, scale_two = step(norm_middle, inputs, gain_two, *parts)

    def expand(normed, gate_role, up_role):
        gate = contract_last(normed, gate_role)
        upward = contract_last(normed, up_role)
        return gate, upward, (gate * jax.nn.sigmoid(gate) * upward).astype(BF16)

    def expand_near(near):
        state["two near"] = step(join, *near)
        state["up near"] = step(expand, state["two near"], gate_role, up_role)

    _, far_two, _, _ = plan.spread(low_two, None, ([], [lambda: wait(up_role)], [expand_near]))
    state["two far"] = step(join, *far_two)
    state["up far"] = step(expand, state["two far"], gate_role, up_role)
    shrink_grad = step(
        product_pairs, state["grad near"], state["up near"][2], state["grad far"], state["up far"][2]
    )
    shrink_summed = lax.psum_scatter(shrink_grad, "dp", scatter_dimension=0, tiled=True)
    shrink_role = wait(shrink_role)

    def back(gate, upward, grad_group, shrink_role):
        sigma = jax.nn.sigmoid(gate)
        swish = gate * sigma
        hidden_grad = plain_product(grad_group, shrink_role)
        gate_grad = hidden_grad * upward * (sigma * (1.0 + gate * (1.0 - sigma)))
        upward_grad = hidden_grad * swish
        return gate_grad.astype(BF16), upward_grad.astype(BF16)

    def back_terms(gate_grad, up_grad, gate_role, up_role):
        return (plain_product(gate_grad, gate_role) + plain_product(up_grad, up_role)).astype(BF16)

    far_back = step(back, *state["up far"][:2], state["grad far"], shrink_role)
    far = step(back_terms, *far_back, gate_role, up_role)

    def near_terms():
        state["back"] = step(back, *state["up near"][:2], state["grad near"], shrink_role)
        return step(back_terms, *state["back"], gate_role, up_role)

    def expand_grad(index):
        return lambda: step(
            product_pairs, state["back"][index], state["two near"], far_back[index], state["two far"]
        )

    parts, (gate_grad, up_grad, far_output, near_output), _ = plan.settle(
        near_terms,
        far,
        rows,
        (
            [],
            [expand_grad(0)],
            [
                expand_grad(1),
                work(product_last, state["up far"][2], shrink_role),
                work(product_last, state["up near"][2], shrink_role),
            ],
        ),
    )
    gate_summed = lax.psum_scatter(gate_grad, "dp", scatter_dimension=0, tiled=True)
    up_summed = lax.psum_scatter(up_grad, "dp", scatter_dimension=0, tiled=True)

    shrink_summed = wait(shrink_summed)

    def shrink_update(gradient, *values):
        gradient = gradient[None].astype(F32)
        return gradient, *adamw(values[0], gradient, *values[1:], RATE, DECAY)

    def shrink_work():
        state["shrink"] = step(
            shrink_update, state["shrink back"], shrink_weight, shrink_moment, shrink_square
        )

    def expand_update(gate, up, weight, moment, square):
        gradient = jnp.stack([gate, up]).astype(F32)
        return gradient, *adamw(weight, gradient, moment, square, RATE, DECAY)

    def back_two(middle, scale, gain, grad_out, own, beside, above):
        grad = own.astype(F32) + beside.astype(F32) + above.astype(F32)
        middle_back, gain_grad = norm_back(middle, scale, gain, grad)
        middle_grad = grad_out + middle_back
        return middle_grad.astype(BF16), middle_grad, gain_grad

    branch_low, middle_grad, gain_two_grad = step(
        back_two, middle, scale_two, gain_two, grad_out, *parts
    )

    def attend_back(name, grads, blocks, places, earlier):
        normed, joint, attended = state["attend " + name]
        return step(
            attend_back_blocks,
            grads,
            blocks,
            mixing_role,
            entry_role,
            joint,
            attended,
            normed,
            state["turn " + name],
            places,
            earlier,
        )

    def order_gains(gain_one_grad, gain_two_grad):
        gains = jnp.stack([gain_one_grad[0], gain_two_grad])
        gains = gains.reshape(2, dp, fsdp, width // (dp * fsdp)).transpose(2, 1, 0, 3)
        return jnp.take(gains, jnp.arange(fsdp) ^ role, axis=0)

    def extra_output(k, came):
        if k == 0:
            return [(far_output, 1)]
        if k == 1:
            return []
        state["sums"] = step(add_low, near_output, came[0][0])
        across = state["sums"][3 * rows :]
        return [(across[: rows // 2], 2), (across[rows // 2 :], 4)]

    def back_near(near_branch):
        state["near back"] = attend_back("near", near_branch, spread_tokens, near_places, [])

    def back_far():
        state["far back"] = attend_back(
            "far", far_branch, far_tokens, far_places, state["near back"][1:]
        )

    _, far_branch, came, _ = plan.spread(
        branch_low,
        None,
        ([], [], [back_near]),
        extra_output,
    )
    gate_summed = wait(gate_summed)
    if plan.short:
        beside, above = step(functools.partial(plan.merge, rows), state["sums"], *came[2])
        parts, _ = window([(beside, 2), (above, 4)], back_far)
        parts = [state["sums"][:rows], *parts]
    else:
        parts, _, _ = plan.settle(lambda: near_output, far_output, rows, ([], [back_far], []))
    layer_output = step(
        lambda *a: sum((value.astype(F32) for value in a[1:]), a[0]).astype(BF16), middle, *parts
    )
    near, far = state["near back"][0], state["far back"][0]
    up_summed = wait(up_summed)

    def lower_sums():
        _, entry_grad, mixing_grad, gain_grad = state["far back"]
        state["entry"], state["mixing"] = step(
            lambda a, b: (low_of(a), low_of(b.T)), entry_grad, mixing_grad
        )
        state["gain"] = step(order_gains, gain_grad, gain_two_grad)

    (got,), _ = window(
        [(far, 1)], lower_sums, store("shrink back", plan.columns_back, shrink_summed)
    )
    entry_grad, mixing_grad, gains = state["entry"], state["mixing"], state["gain"]
    if whole_heads:
        mixing_summed = lax.psum_scatter(mixing_grad, "dp", scatter_dimension=0, tiled=True)
        entry_gradient = lax.psum_scatter(
            entry_grad.reshape(3, dp * HEAD, width), "dp", scatter_dimension=1, tiled=True
        )
    else:
        entry_full = lax.dynamic_update_slice_in_dim(
            jnp.zeros((3, width, width), BF16),
            entry_grad.reshape(3, span, width),
            role * span,
            axis=1,
        )
        mixing_full = lax.dynamic_update_slice_in_dim(
            jnp.zeros((width, width), BF16), mixing_grad, role * span, axis=1
        )
        entry_gradient = lax.psum_scatter(entry_full, AXES, scatter_dimension=1, tiled=True)
        mixing_summed = lax.psum_scatter(mixing_full, AXES, scatter_dimension=0, tiled=True)

    def mixing_update(gradient, *values):
        if whole_heads:
            gradient = plan.columns_back(gradient)
        gradient = gradient[None].astype(F32)
        return gradient, *adamw(values[0], gradient, *values[1:], MIXING_RATE, DECAY)

    parts, _, gains = plan.settle(
        lambda: near,
        far,
        rows,
        (
            [],
            [lambda: shrink_work()],
            [
                store(
                    "expand",
                    expand_update,
                    gate_summed,
                    up_summed,
                    expand_weight,
                    expand_moment,
                    expand_square,
                ),
                store(
                    "mixing new",
                    mixing_update,
                    mixing_summed,
                    mixing_weight,
                    mixing_moment,
                    mixing_square,
                ),
            ],
        ),
        gains,
        got,
    )
    mixing_gradient, *mixing_new = state["mixing new"]
    def back_input(inputs, gain, middle_grad, *parts):
        scale = lax.rsqrt(jnp.mean(inputs * inputs, axis=-1, keepdims=True) + EPS)
        grad = sum(value.astype(F32) for value in parts)
        return middle_grad + norm_back(inputs, scale, gain, grad)[0]

    input_gradient = step(back_input, inputs, gain_one, middle_grad, *parts)

    def order_dp(gains):
        return jnp.take(gains[0], jnp.arange(dp) ^ lax.axis_index("dp"), axis=0)

    gains = step(order_dp, gains)
    for bit in reversed([1 << k for k in range((dp - 1).bit_length())]):
        (got,), _ = window([(gains[bit:], -bit)])
        gains = step(lambda a, b: a[:bit] + b, gains, got)
    gain_grads = gains[0]
    attention_gradient, feedforward_gradient = gain_grads[:1], gain_grads[1:]
    shrink_gradient, *shrink_new = state["shrink"]
    expand_gradient, *expand_new = state["expand"]
    entry_gradient = entry_gradient.astype(F32)
    entry_new = adamw(entry_weight, entry_gradient, entry_moment, entry_square, RATE, DECAY)
    attention_new = adamw(
        attention_gain, attention_gradient, attention_moment, attention_square, GAIN_RATE, 0.0
    )
    feedforward_new = adamw(
        feedforward_gain,
        feedforward_gradient,
        feedforward_moment,
        feedforward_square,
        GAIN_RATE,
        0.0,
    )
    return (
        layer_output,
        input_gradient,
        entry_gradient,
        mixing_gradient,
        attention_gradient,
        expand_gradient,
        shrink_gradient,
        feedforward_gradient,
        entry_new[0],
        mixing_new[0],
        attention_new[0],
        expand_new[0],
        shrink_new[0],
        feedforward_new[0],
        entry_new[1],
        entry_new[2],
        mixing_new[1],
        mixing_new[2],
        attention_new[1],
        attention_new[2],
        expand_new[1],
        expand_new[2],
        shrink_new[1],
        shrink_new[2],
        feedforward_new[1],
        feedforward_new[2],
    )


def solution(mesh):
    placed = (
        P(("dp", "fsdp"), None),
        P(("dp", "fsdp")),
        P(("dp", "fsdp"), None),
        P(None, ("dp", "fsdp"), None),
        P(None, ("dp", "fsdp"), None),
        P(None, ("dp", "fsdp")),
        P(None, ("dp", "fsdp"), None),
        P(None, ("dp", "fsdp"), None),
        P(None, ("dp", "fsdp")),
        P(None, ("dp", "fsdp"), None),
        P(None, ("dp", "fsdp"), None),
        P(None, ("dp", "fsdp"), None),
        P(None, ("dp", "fsdp"), None),
        P(None, ("dp", "fsdp")),
        P(None, ("dp", "fsdp")),
        P(None, ("dp", "fsdp"), None),
        P(None, ("dp", "fsdp"), None),
        P(None, ("dp", "fsdp"), None),
        P(None, ("dp", "fsdp"), None),
        P(None, ("dp", "fsdp")),
        P(None, ("dp", "fsdp")),
    )
    return jax.shard_map(
        functools.partial(local, mesh.shape["dp"], mesh.shape["fsdp"]),
        mesh=mesh,
        in_specs=placed,
        out_specs=(
            P(("dp", "fsdp"), None),
            P(("dp", "fsdp"), None),
            P(None, ("dp", "fsdp"), None),
            P(None, ("dp", "fsdp"), None),
            P(None, ("dp", "fsdp")),
            P(None, ("dp", "fsdp"), None),
            P(None, ("dp", "fsdp"), None),
            P(None, ("dp", "fsdp")),
            P(None, ("dp", "fsdp"), None),
            P(None, ("dp", "fsdp"), None),
            P(None, ("dp", "fsdp")),
            P(None, ("dp", "fsdp"), None),
            P(None, ("dp", "fsdp"), None),
            P(None, ("dp", "fsdp")),
            P(None, ("dp", "fsdp"), None),
            P(None, ("dp", "fsdp"), None),
            P(None, ("dp", "fsdp"), None),
            P(None, ("dp", "fsdp"), None),
            P(None, ("dp", "fsdp")),
            P(None, ("dp", "fsdp")),
            P(None, ("dp", "fsdp"), None),
            P(None, ("dp", "fsdp"), None),
            P(None, ("dp", "fsdp"), None),
            P(None, ("dp", "fsdp"), None),
            P(None, ("dp", "fsdp")),
            P(None, ("dp", "fsdp")),
        ),
        check_vma=False,
    )
```

```python
import functools

import jax
import jax.numpy as jnp
from jax import lax
from jax.experimental import pallas as pl
from jax.experimental.pallas import tpu as pltpu
from jax.sharding import PartitionSpec as P

HEADS = 32
HEAD = 64
STEP = 3


EPS = 1e-05
THETA = 130000.0
RATE = 0.01
MIXING_RATE = 0.04
GAIN_RATE = 0.3
BETA_ONE = 0.9
BETA_TWO = 0.95
ADAM_EPS = 1e-08
DECAY = 0.1


def contract_last(left, right):
    return lax.dot_general(
        left, right, (((1,), (1,)), ((), ())), preferred_element_type=jnp.float32
    )


def contract_first(left, right):
    return lax.dot_general(
        left, right, (((0,), (0,)), ((), ())), preferred_element_type=jnp.float32
    )


def plain_product(left, right):
    return jnp.dot(left, right, preferred_element_type=jnp.float32)


def rope_tables(positions):
    half = HEAD // 2
    freq = THETA ** (-2.0 * jnp.arange(half, dtype=jnp.float32) / HEAD)
    angle = positions.astype(jnp.float32)[:, None] * freq[None, :]
    return (jnp.cos(angle), jnp.sin(angle))


def norm_back(value, scale, gain, grad):
    weighted = grad * gain
    inner = jnp.mean(weighted * value, axis=-1, keepdims=True)
    back = scale * weighted - value * (scale * scale * scale) * inner
    return (back, jnp.sum(grad * value * scale, axis=0))


def adamw(weight, gradient, moment, square, rate, decay):
    moment_new = BETA_ONE * moment + (1.0 - BETA_ONE) * gradient
    square_new = BETA_TWO * square + (1.0 - BETA_TWO) * gradient * gradient
    corrected = moment_new / (1.0 - BETA_ONE**STEP)
    spread = jnp.sqrt(square_new / (1.0 - BETA_TWO**STEP)) + ADAM_EPS
    return (weight - rate * (corrected / spread + decay * weight), moment_new, square_new)


AXES = ("dp", "fsdp")
VMEM_BYTES = 56 * 2**20
BF16 = jnp.bfloat16
F32 = jnp.float32


def add_low(*values):
    return sum(value.astype(F32) for value in values).astype(BF16)


def probs_of(left, right, places_down, places_across, turned):
    rows = right.shape[0]
    down = lax.broadcasted_iota(jnp.int32, (rows, rows), 0)
    across = lax.broadcasted_iota(jnp.int32, (rows, rows), 1)
    earlier = down <= across if turned else across <= down
    visible = (places_down - places_across == down - across) & earlier
    raw = contract_last(left, right).reshape(-1, rows, rows)
    scores = jnp.where(visible[None], raw * (HEAD ** (-0.5)), -1e30)
    axis = 1 if turned else 2
    weights = jnp.exp(scores - jnp.max(scores, axis=axis, keepdims=True))
    return weights * (1.0 / jnp.sum(weights, axis=axis, keepdims=True))


def by_head(value):
    head = lax.broadcasted_iota(jnp.int32, value.shape, 1) // HEAD
    none = jnp.zeros_like(value)
    return jnp.concatenate(
        [jnp.where(head == h, value, none) for h in range(value.shape[1] // HEAD)]
    )


def own_columns(value, rows):
    head = lax.broadcasted_iota(jnp.int32, (rows, value.shape[1]), 1) // HEAD
    total = value[:rows]
    for h in range(1, value.shape[1] // HEAD):
        total = jnp.where(head == h, value[h * rows : (h + 1) * rows], total)
    return total


def swap_halves(value):
    columns = value.shape[1]
    half = HEAD // 2
    lane = lax.broadcasted_iota(jnp.int32, value.shape, 1) % HEAD
    return jnp.where(
        lane < half, pltpu.roll(value, columns - half, 1), pltpu.roll(value, half, 1)
    )


def attend_kernel(group, *refs):
    blocks, refs = refs[:group], refs[group:]
    gain, weight, cosine, sine, down, across, normed, joint, attended, held = refs
    for k in range(group):

        @pl.when(pl.program_id(0) == k)
        def _():
            held[...] = blocks[k][...]

    value = held[...].astype(F32)
    scale = lax.rsqrt(jnp.mean(value * value, axis=-1, keepdims=True) + EPS)
    normed[...] = (value * scale * gain[...]).astype(BF16)
    mixed = contract_last(normed[...], weight[...])
    span = mixed.shape[1] // 3
    for part in range(2):
        piece = mixed[:, part * span : (part + 1) * span]
        joint[:, part * span : (part + 1) * span] = (
            piece * cosine[...] + swap_halves(piece) * sine[...]
        ).astype(BF16)
    joint[:, 2 * span :] = mixed[:, 2 * span :].astype(BF16)
    query, keys, values = (joint[:, part * span : (part + 1) * span] for part in range(3))
    rows = query.shape[0]
    probs = probs_of(by_head(query), keys, down[0, :, :1], across[0, :1], False).astype(BF16)
    found = plain_product(probs.reshape(-1, rows), values)
    attended[...] = own_columns(found, rows).astype(BF16)


def attend_blocks(blocks, gain, weight, cosine, sine, down, across):
    group = len(blocks)
    rows, width = blocks[0].shape
    span = weight.shape[0] // 3
    whole = lambda *shape: pl.BlockSpec(shape, lambda i: (0,) * len(shape))
    by_row = lambda columns: pl.BlockSpec((rows, columns), lambda i: (i, 0))
    return pl.pallas_call(
        functools.partial(attend_kernel, group),
        grid=(group,),
        in_specs=[whole(rows, width)] * group
        + [whole(1, width), whole(3 * span, width), by_row(span), by_row(span)]
        + [
            pl.BlockSpec((1, rows, 128), lambda i: (i, 0, 0)),
            pl.BlockSpec((1, 8, rows), lambda i: (i, 0, 0)),
        ],
        out_specs=[by_row(width), by_row(3 * span), by_row(span)],
        out_shape=[
            jax.ShapeDtypeStruct((group * rows, columns), BF16)
            for columns in (width, 3 * span, span)
        ],
        scratch_shapes=[pltpu.VMEM((rows, width), BF16)],
        compiler_params=pltpu.CompilerParams(vmem_limit_bytes=VMEM_BYTES),
    )(*blocks, gain[None], weight, cosine, sine, down, across)


def attend_back_kernel(group, first, *refs):
    grads, blocks, refs = refs[:group], refs[group : 2 * group], refs[2 * group :]
    mixing, weight, joint, attended, normed, cosine, sine, down, across = refs[:9]
    earlier, refs = (None, refs[9:]) if first else (refs[9:12], refs[12:])
    terms, entry_sum, mixing_sum, gain_sum, held, tokens, back, mixing_total = refs
    step = pl.program_id(0)
    for k in range(group):

        @pl.when(step == k)
        def _():
            held[...] = grads[k][...]
            tokens[...] = blocks[k][...]

    @pl.when(step == 0)
    def _():
        for k, sums in ((1, mixing_total), (2, gain_sum)):
            sums[...] = jnp.zeros_like(sums) if first else earlier[k][...]

    rows = held.shape[0]
    here = pl.ds(pl.multiple_of(step * rows, rows), rows)
    span = joint.shape[1] // 3
    query, keys, values = (joint[:, part * span : (part + 1) * span] for part in range(3))
    grad = plain_product(held[...], mixing[...]).astype(BF16)
    key_heads = by_head(keys)
    probs = probs_of(key_heads, query, down[0, :, :1], across[0, :1], True)
    prob_grad = contract_last(by_head(values), grad).reshape(probs.shape)
    delta = jnp.sum(probs * prob_grad, axis=1, keepdims=True)
    score_grad = (probs * (prob_grad - delta)).astype(BF16).reshape(-1, rows)
    query_grad = contract_first(score_grad, key_heads)
    key_grad = own_columns(plain_product(score_grad, query), rows)
    value_grad = own_columns(plain_product(probs.astype(BF16).reshape(-1, rows), grad), rows)
    for part, value in enumerate((query_grad, key_grad)):
        value = value * (HEAD ** (-0.5))
        back[here, part * span : (part + 1) * span] = (
            value * cosine[...] - swap_halves(value) * sine[...]
        ).astype(BF16)
    back[here, 2 * span :] = value_grad.astype(BF16)
    term = plain_product(back[here, :], weight[...])
    terms[...] = term.astype(BF16)
    value = tokens[...].astype(F32)
    scale = lax.rsqrt(jnp.mean(value * value, axis=-1, keepdims=True) + EPS)
    gain_sum[...] += jnp.sum(term * (value * scale), axis=0, keepdims=True)
    mixing_total[...] += contract_first(attended[...], held[...])

    @pl.when(step == group - 1)
    def _():
        for part in range(3):
            part = slice(part * span, (part + 1) * span)
            found = contract_first(back[:, part], normed[...])
            if not first:
                found += earlier[0][part, :]
            entry_sum[part, :] = found.astype(entry_sum.dtype)
        mixing_sum[...] = mixing_total[...].astype(mixing_sum.dtype)


def attend_back_blocks(grads, blocks, mixing, weight, joint, attended, normed, turn, earlier):
    group = len(blocks)
    rows, width = blocks[0].shape
    span = weight.shape[0] // 3
    whole = lambda *shape: pl.BlockSpec(shape, lambda i: (0,) * len(shape))
    by_row = lambda columns: pl.BlockSpec((rows, columns), lambda i: (i, 0))
    sums = [(3 * span, width), (span, width), (1, width)]
    return pl.pallas_call(
        functools.partial(attend_back_kernel, group, not earlier),
        grid=(group,),
        in_specs=[whole(rows, width)] * (2 * group)
        + [whole(width, span), whole(3 * span, width)]
        + [by_row(3 * span), by_row(span), whole(group * rows, width), by_row(span), by_row(span)]
        + [
            pl.BlockSpec((1, rows, 128), lambda i: (i, 0, 0)),
            pl.BlockSpec((1, 8, rows), lambda i: (i, 0, 0)),
        ]
        + [whole(*shape) for shape in sums if earlier],
        out_specs=[by_row(width)] + [whole(*shape) for shape in sums],
        out_shape=[jax.ShapeDtypeStruct((group * rows, width), BF16)]
        + [
            jax.ShapeDtypeStruct(shape, BF16 if earlier and shape[0] > 1 else F32) for shape in sums
        ],
        scratch_shapes=[
            pltpu.VMEM((rows, width), BF16),
            pltpu.VMEM((rows, width), BF16),
            pltpu.VMEM((group * rows, 3 * span), BF16),
            pltpu.VMEM((span, width), F32),
        ],
        compiler_params=pltpu.CompilerParams(vmem_limit_bytes=VMEM_BYTES),
    )(
        *grads,
        *blocks,
        mixing,
        weight,
        joint,
        attended,
        normed,
        *turn,
        *earlier,
    )


def turn_tables(places, heads):
    cosine, sine = rope_tables(places.reshape(-1))
    return (
        jnp.tile(jnp.concatenate([cosine, cosine], axis=1), (1, heads)),
        jnp.tile(jnp.concatenate([-sine, sine], axis=1), (1, heads)),
        jnp.broadcast_to(places[:, :, None], (*places.shape, 128)),
        jnp.broadcast_to(places[:, None, :], (places.shape[0], 8, places.shape[1])),
    )


def expand_kernel(group, *refs):
    blocks, weight, joined, gate, upward, hidden = refs[:group], *refs[group:]
    rows = blocks[0].shape[0]

    @pl.when(pl.program_id(0) == 0)
    def _():
        for k in range(group):
            joined[k * rows : (k + 1) * rows, :] = blocks[k][...]

    gate[...] = contract_last(joined[...], weight[0])
    upward[...] = contract_last(joined[...], weight[1])
    hidden[...] = (gate[...] * jax.nn.sigmoid(gate[...]) * upward[...]).astype(BF16)


def expand_blocks(blocks, weight):
    group = len(blocks)
    rows, width = blocks[0].shape
    units = weight.shape[1]
    tile = min(units, 256)
    by_unit = pl.BlockSpec((group * rows, tile), lambda j: (0, j))
    shape = group * rows, units
    return pl.pallas_call(
        functools.partial(expand_kernel, group),
        grid=(units // tile,),
        in_specs=[pl.BlockSpec((rows, width), lambda j: (0, 0))] * group
        + [pl.BlockSpec((2, tile, width), lambda j: (0, j, 0))],
        out_specs=[pl.BlockSpec((group * rows, width), lambda j: (0, 0))] + [by_unit] * 3,
        out_shape=[
            jax.ShapeDtypeStruct((group * rows, width), BF16),
            jax.ShapeDtypeStruct(shape, F32),
            jax.ShapeDtypeStruct(shape, F32),
            jax.ShapeDtypeStruct(shape, BF16),
        ],
        compiler_params=pltpu.CompilerParams(vmem_limit_bytes=VMEM_BYTES),
    )(*blocks, weight)


def expand_back_kernel(tiles, grads, gate, upward, shrink, weight, gate_grad, up_grad, terms, both):
    step = pl.program_id(0)
    tile = gate.shape[1]

    @pl.when(step < tiles)
    def _():
        sigma = jax.nn.sigmoid(gate[...])
        swish = gate[...] * sigma
        hidden_grad = plain_product(grads[...], shrink[...])
        slope = sigma * (1.0 + gate[...] * (1.0 - sigma))
        gate_grad[...] = (hidden_grad * upward[...] * slope).astype(BF16)
        up_grad[...] = (hidden_grad * swish).astype(BF16)
        both[step] = gate_grad[...]
        both[tiles + step] = up_grad[...]

    @pl.when(step >= tiles)
    def _():
        total = jnp.zeros(terms.shape, F32)
        for k in range(2 * tiles):
            part, first = k // tiles, k % tiles * tile
            total += plain_product(both[k], weight[part, first : first + tile, :])
        terms[...] = total.astype(BF16)


def expand_back_blocks(grads, gate, upward, shrink, weight):
    rows, width = grads.shape
    units = gate.shape[1]
    tile = min(units, 256)
    tiles = units // tile
    cuts = 4
    early = lambda j: jnp.minimum(j, tiles - 1)
    late = lambda j: jnp.maximum(j - tiles, 0)
    by_unit = pl.BlockSpec((rows, tile), lambda j: (0, early(j)))
    return pl.pallas_call(
        functools.partial(expand_back_kernel, tiles),
        grid=(tiles + cuts,),
        in_specs=[
            pl.BlockSpec((rows, width), lambda j: (0, 0)),
            by_unit,
            by_unit,
            pl.BlockSpec((width, tile), lambda j: (0, early(j))),
            pl.BlockSpec((2, units, width // cuts), lambda j: (0, 0, late(j))),
        ],
        out_specs=[
            by_unit,
            by_unit,
            pl.BlockSpec((rows, width // cuts), lambda j: (0, late(j))),
        ],
        out_shape=[
            jax.ShapeDtypeStruct((rows, units), BF16),
            jax.ShapeDtypeStruct((rows, units), BF16),
            jax.ShapeDtypeStruct((rows, width), BF16),
        ],
        scratch_shapes=[pltpu.VMEM((2 * tiles, rows, tile), BF16)],
        compiler_params=pltpu.CompilerParams(vmem_limit_bytes=VMEM_BYTES),
    )(grads, gate, upward, shrink, weight)


class Plan:
    def __init__(self, dp, fsdp):
        self.dp, self.fsdp = dp, fsdp
        self.clock = None
        self.bits = [1 << k for k in range(1, (fsdp - 1).bit_length())] + [1]
        self.short = fsdp == 8

    def tie(self, values):
        if self.clock is None:
            return tuple(values)
        return lax.optimization_barrier((tuple(values), self.clock))[0]

    def step(self, work, *values):
        found = work(*self.tie(values))
        self.clock = jax.tree.leaves(found)
        return found

    def window(self, sends, *works):
        values = self.tie([value for value, _ in sends])
        came = []
        for value, (_, mask) in zip(values, sends):
            axis, count = ("fsdp", self.fsdp) if mask > 0 else ("dp", self.dp)
            pairs = [(i, i ^ abs(mask)) for i in range(count)]
            came.append(lax.ppermute(value, axis, pairs))
        gave, done = [], []
        for work in works:
            gave.append(work())
            done += self.clock
        came, self.clock = lax.optimization_barrier((came, done or came))
        return came, gave

    def wait(self, value):
        self.clock = [*self.clock, value]
        return value

    def merge(self, rows, sums, first, second):
        half = rows // 2
        beside, above = sums[rows : 2 * rows], sums[2 * rows : 3 * rows]
        return (
            jnp.concatenate([beside[:half], add_low(beside[half:], second)]),
            jnp.concatenate([add_low(above[:half], first), above[half:]]),
        )

    def spread(self, block, marks=None, works=((), (), ()), extra=None):
        small = marks is not None
        gave, more = [], []

        def added(k):
            return [] if extra is None else extra(k, more)

        if self.short:
            half = block.shape[0] // 2
            (beside, above, other, *got), found = self.window(
                [(block, 2), (block, 4), (block, 1)] + [(marks, 2)] * small + added(0), *works[0]
            )
            gave += found
            more.append(got)
            if small:
                marks = self.step(lambda a, b: jnp.concatenate([a, b]), marks, *got)
            upper, lower, pair = self.step(
                lambda a, b: (a[:half], b[half:], jnp.concatenate([b, a])), above, beside
            )
            (first, second, pair, *got), found = self.window(
                [(upper, 2), (lower, 4), (pair, 1)] + [(marks, 4)] * small + added(1), *works[1]
            )
            gave += found
            more.append(got)
            across = self.step(lambda a, b: jnp.concatenate([a, b]), first, second)
            if small:
                marks = self.step(lambda a, b: jnp.concatenate([a, b]), marks, *got)
            near = [block, beside, above, across]
            (far, *got), found = self.window(
                [(across, 1)] + [(marks, 1)] * small + added(2),
                *[functools.partial(w, near) for w in works[2]],
            )
            more.append(got)
            size = block.shape[0]
            got = got if extra is None else more
            return near, [other, pair[:size], pair[size:], far], (marks, *got), gave + found
        near = [block]
        for bit in self.bits[:-1]:
            got, _ = self.window([(piece, bit) for piece in near] + [(marks, bit)] * small)
            if small:
                marks = jnp.concatenate([marks, got[-1]])
            near = near + got[: len(near)]
        for work in [*works[0], *works[1]]:
            gave.append(work())
        got, found = self.window(
            [(piece, 1) for piece in near] + [(marks, 1)] * small,
            *[functools.partial(w, near) for w in works[2]],
        )
        return near, got[: len(near)], (marks, *got[len(near) :]), gave + found

    def settle(self, near, far, rows, works=((), (), ()), small=None, got=None, finish=None):
        gave = []

        def sends(bit):
            return [] if small is None else [(small[bit:], bit)]

        def sum_small(got, bit):
            if got:
                return self.step(lambda a, b: a[:bit] + b, small, *got)
            return None

        if not self.short:
            terms = jnp.concatenate([near(), far])
            for work in [*works[0], *works[1], *works[2]]:
                gave.append(work())
            for bit in reversed(self.bits):
                size = terms.shape[0] // 2
                if got is None:
                    (got,), _ = self.window([(terms[size:], bit)])
                terms = self.step(add_low, terms[:size], got)
                got = None
            if small is not None:
                for bit in sorted(self.bits, reverse=True):
                    small = sum_small(self.window(sends(bit))[0], bit)
            parts = terms, jnp.zeros_like(terms), jnp.zeros_like(terms)
            if finish is not None:
                finish(*parts)
            return parts, gave, small
        half = rows // 2
        if got is None:
            (got,), (near, *found) = self.window([(far, 1)], near, *works[0])
            gave += found
        else:
            near = near()
        sums = self.step(add_low, near, got)
        across = sums[3 * rows :]
        (first, second, *more), found = self.window(
            [(across[:half], 2), (across[half:], 4)] + sends(4), *works[1]
        )
        gave += found
        small = sum_small(more, 4)

        beside, above = self.step(functools.partial(self.merge, rows), sums, first, second)
        (beside, above, *more), found = self.window([(beside, 2), (above, 4)] + sends(2), *works[2])
        small = sum_small(more, 2)
        if small is not None:
            (more,), _ = self.window(sends(1), lambda: finish(sums[:rows], beside, above))
            small = sum_small([more], 1)
        return (sums[:rows], beside, above), gave + found, small

    def columns_split(self, shard):
        rows, columns = shard.shape
        width = columns // (self.dp * self.fsdp)
        blocks = shard.reshape(rows, self.dp, self.fsdp, width).transpose(2, 0, 1, 3)
        return blocks.reshape(self.fsdp, rows, self.dp * width)

    def exchange(self, blocks):
        return lax.all_to_all(blocks, "fsdp", 0, 0, tiled=True)

    def columns_back(self, *sums):
        rows = sums[0].shape[0] // self.fsdp
        blocks = [value.reshape(self.fsdp, rows, -1) for value in sums]
        blocks = self.exchange(jnp.concatenate(blocks, axis=-1))
        found, last = [], 0
        for value in sums:
            first, last = last, last + value.shape[1]
            block = blocks[..., first:last].reshape(self.fsdp, rows, self.dp, -1)
            found.append(block.transpose(1, 2, 0, 3).reshape(rows, self.fsdp * value.shape[1]))
        return found


def local(
    dp,
    fsdp,
    tokens,
    positions,
    cotangent,
    entry_weight,
    mixing_weight,
    attention_gain,
    expand_weight,
    shrink_weight,
    feedforward_gain,
    entry_moment,
    entry_square,
    mixing_moment,
    mixing_square,
    attention_moment,
    attention_square,
    expand_moment,
    expand_square,
    shrink_moment,
    shrink_square,
    feedforward_moment,
    feedforward_square,
):
    plan = Plan(dp, fsdp)
    step, window, wait = plan.step, plan.window, plan.wait
    rows = tokens.shape[0]
    width = tokens.shape[1]
    group = fsdp // 2
    whole_heads = entry_weight.shape[1] == HEAD
    heads = HEADS // fsdp
    span = heads * HEAD
    factor = HEAD ** (-0.5)
    state = {}

    def work(call, *values):
        return lambda *_: step(call, *values)

    def store(name, call, *values):
        def run(*_):
            state[name] = step(call, *values)

        return run

    def low_of(value):
        return value.astype(BF16)

    join = lambda *a: jnp.concatenate(a)
    product_last = lambda a, b: contract_last(a, b).astype(BF16)
    product_plain = lambda a, b: plain_product(a, b).astype(BF16)

    def product_pairs(a, b, c, d):
        return (contract_first(a, b) + contract_first(c, d)).astype(BF16)

    entry_low = step(low_of, entry_weight)
    role = lax.axis_index("fsdp")
    if whole_heads:
        entry_role = lax.all_gather(entry_low, "dp", axis=1, tiled=True)
    else:
        entry_all = lax.all_gather(entry_low, AXES, axis=1, tiled=True)
        entry_role = lax.dynamic_slice_in_dim(entry_all, role * span, span, axis=1)

    def gains_dp(*gains):
        gains = jnp.concatenate(gains).astype(BF16)[:, None]
        return lax.all_gather(gains, "dp", axis=1, tiled=True)

    def gains_fsdp(gains):
        gains = lax.all_gather(gains[:, :, None], "fsdp", axis=2, tiled=True)
        return gains.reshape(2, width).astype(F32)

    def columns_work(shrink_low, mixing_low):
        blocks = plan.exchange(
            jnp.concatenate([plan.columns_split(shrink_low), plan.columns_split(mixing_low)], -1)
        )
        size = shrink_low.shape[1] // fsdp
        return blocks[..., :size], blocks[..., size:]

    spread_tokens, far_tokens, (near_places, far_places), _ = plan.spread(
        tokens,
        positions[None],
        (
            [
                store("mixing_low", low_of, mixing_weight[0]),
                store("shrink_low", low_of, shrink_weight[0]),
                store("gains_dp", gains_dp, attention_gain, feedforward_gain),
                lambda: state.update(
                    columns=step(columns_work, state["shrink_low"], state["mixing_low"])
                ),
            ],
            [
                store("expand_low", low_of, expand_weight),
                lambda: state.update(gains=step(gains_fsdp, state["gains_dp"])),
            ],
            [],
        ),
    )
    gain_one, gain_two = state["gains"][0], state["gains"][1]
    shrink_blocks, mixing_blocks = state["columns"]
    if whole_heads:
        mixing_role = lax.all_gather(mixing_blocks, "dp", axis=0, tiled=True).reshape(width, span)
    else:
        mixing_all = lax.all_gather(state["mixing_low"], AXES, axis=0, tiled=True)
        mixing_role = lax.dynamic_slice_in_dim(mixing_all, role * span, span, axis=1)
    expand_role = lax.all_gather(state["expand_low"], "dp", axis=1, tiled=True)
    shrink_role = lax.all_gather(shrink_blocks, "dp", axis=0, tiled=True).reshape(width, -1)

    inputs = tokens.astype(F32)
    live = (positions >= 0).astype(F32)[:, None]
    grad_out = cotangent.astype(F32) * live
    grad_low = step(low_of, grad_out)
    entry_role = wait(entry_role).reshape(3 * span, width)
    state["turn near"] = step(lambda a: turn_tables(a, heads), near_places)
    state["turn far"] = step(lambda a: turn_tables(a, heads), far_places)

    def attend_work(name, blocks):
        def run(*_):
            state["attend " + name] = step(
                attend_blocks, blocks, gain_one, entry_role, *state["turn " + name]
            )

        return run

    near_grad, far_grad, _, _ = plan.spread(
        grad_low,
        None,
        (
            [attend_work("far", far_tokens)],
            [
                attend_work("near", spread_tokens),
            ],
            [],
        ),
    )
    mixing_role = wait(mixing_role)
    far = step(product_last, state["attend far"][2], mixing_role)
    near = work(product_last, state["attend near"][2], mixing_role)
    parts, _, _ = plan.settle(
        near, far, rows, ([], [store("grad near", join, *near_grad)], [store("grad far", join, *far_grad)])
    )

    def norm_middle(inputs, gain, own, beside, above):
        middle = inputs + own.astype(F32) + beside.astype(F32) + above.astype(F32)
        scale = lax.rsqrt(jnp.mean(middle * middle, axis=-1, keepdims=True) + EPS)
        return (middle * scale * gain).astype(BF16), middle, scale

    low_two, middle, scale_two = step(norm_middle, inputs, gain_two, *parts)

    def expand_near(near):
        state["up near"] = step(expand_blocks, near, expand_role)

    _, far_two, _, _ = plan.spread(
        low_two, None, ([], [lambda: wait(expand_role)], [expand_near])
    )
    state["up far"] = step(expand_blocks, far_two, expand_role)
    shrink_grad = step(
        product_pairs, state["grad near"], state["up near"][3], state["grad far"], state["up far"][3]
    )
    shrink_summed = lax.psum_scatter(shrink_grad, "dp", scatter_dimension=0, tiled=True)
    shrink_role = wait(shrink_role)

    def expand_back(name):
        return step(
            expand_back_blocks,
            state["grad " + name],
            *state["up " + name][1:3],
            shrink_role,
            expand_role,
        )

    far_back = expand_back("far")
    far = far_back[2]

    def near_terms():
        state["back"] = expand_back("near")
        return state["back"][2]

    def expand_grad(index):
        return lambda: step(
            product_pairs, state["back"][index], state["up near"][0], far_back[index], state["up far"][0]
        )

    parts, (gate_grad, up_grad, far_output, near_output), _ = plan.settle(
        near_terms,
        far,
        rows,
        (
            [],
            [expand_grad(0)],
            [
                expand_grad(1),
                work(product_last, state["up far"][3], shrink_role),
                work(product_last, state["up near"][3], shrink_role),
            ],
        ),
    )
    gate_summed = lax.psum_scatter(gate_grad, "dp", scatter_dimension=0, tiled=True)
    up_summed = lax.psum_scatter(up_grad, "dp", scatter_dimension=0, tiled=True)

    shrink_summed = wait(shrink_summed)

    def expand_update(gate, up, weight, moment, square):
        gradient = jnp.stack([gate, up]).astype(F32)
        return gradient, *adamw(weight, gradient, moment, square, RATE, DECAY)

    def back_two(middle, scale, gain, grad_out, own, beside, above):
        grad = own.astype(F32) + beside.astype(F32) + above.astype(F32)
        middle_back, gain_grad = norm_back(middle, scale, gain, grad)
        middle_grad = grad_out + middle_back
        return middle_grad.astype(BF16), middle_grad, gain_grad

    branch_low, middle_grad, gain_two_grad = step(
        back_two, middle, scale_two, gain_two, grad_out, *parts
    )

    def attend_back(name, grads, blocks, earlier):
        normed, joint, attended = state["attend " + name]
        return step(
            attend_back_blocks,
            grads,
            blocks,
            mixing_role,
            entry_role,
            joint,
            attended,
            normed,
            state["turn " + name],
            earlier,
        )

    def order_gains(gain_one_grad, gain_two_grad):
        gains = jnp.stack([gain_one_grad[0], gain_two_grad])
        gains = gains.reshape(2, dp, fsdp, width // (dp * fsdp)).transpose(2, 1, 0, 3)
        return jnp.take(gains, jnp.arange(fsdp) ^ role, axis=0)

    def extra_output(k, came):
        if k == 0:
            return [(far_output, 1)]
        if k == 1:
            state["came"] = came[0][0]
            return []
        across = state["sums"][3 * rows :]
        return [(across[: rows // 2], 2), (across[rows // 2 :], 4)]

    def back_near(near_branch):
        state["near back"] = attend_back("near", near_branch, spread_tokens, [])

    def back_far():
        state["far back"] = attend_back(
            "far", far_branch, far_tokens, state["near back"][1:]
        )

    _, far_branch, came, _ = plan.spread(
        branch_low,
        None,
        (
            [],
            [lambda: state.update(sums=step(add_low, near_output, state["came"]))] * plan.short,
            [back_near],
        ),
        extra_output,
    )
    gate_summed = wait(gate_summed)
    if plan.short:
        beside, above = step(functools.partial(plan.merge, rows), state["sums"], *came[3])
        parts, _ = window([(beside, 2), (above, 4)], back_far)
        parts = [state["sums"][:rows], *parts]
    else:
        parts, _, _ = plan.settle(lambda: near_output, far_output, rows, ([], [back_far], []))
    layer_output = step(
        lambda *a: sum((value.astype(F32) for value in a[1:]), a[0]).astype(BF16), middle, *parts
    )
    near, far = state["near back"][0], state["far back"][0]
    up_summed = wait(up_summed)

    _, entry_grad, mixing_grad, gain_grad = state["far back"]
    mixing_grad = step(lambda a: a.T, mixing_grad)
    if whole_heads:
        mixing_summed = lax.psum_scatter(mixing_grad, "dp", scatter_dimension=0, tiled=True)
        entry_gradient = lax.psum_scatter(
            entry_grad.reshape(3, dp * HEAD, width), "dp", scatter_dimension=1, tiled=True
        )
    else:
        entry_full = lax.dynamic_update_slice_in_dim(
            jnp.zeros((3, width, width), BF16),
            entry_grad.reshape(3, span, width),
            role * span,
            axis=1,
        )
        mixing_full = lax.dynamic_update_slice_in_dim(
            jnp.zeros((width, width), BF16), mixing_grad, role * span, axis=1
        )
        entry_gradient = lax.psum_scatter(entry_full, AXES, scatter_dimension=1, tiled=True)
        mixing_summed = lax.psum_scatter(mixing_full, AXES, scatter_dimension=0, tiled=True)

    gains = step(order_gains, gain_grad, gain_two_grad)
    (got,), ((shrink_back,),) = window([(far, 1)], work(plan.columns_back, shrink_summed))

    def back_input(inputs, gain, middle_grad, *parts):
        scale = lax.rsqrt(jnp.mean(inputs * inputs, axis=-1, keepdims=True) + EPS)
        grad = sum(value.astype(F32) for value in parts)
        return middle_grad + norm_back(inputs, scale, gain, grad)[0]

    def finish(*parts):
        state["input"] = step(back_input, inputs, gain_one, middle_grad, *parts)

    def columns_update(shrink_back, mixing_summed, shrink, mixing):
        if whole_heads:
            (mixing_summed,) = plan.columns_back(mixing_summed)
        found = []
        for gradient, values, rate in (
            (shrink_back, shrink, RATE),
            (mixing_summed, mixing, MIXING_RATE),
        ):
            gradient = gradient[None].astype(F32)
            found.append((gradient, adamw(values[0], gradient, *values[1:], rate, DECAY)))
        return found

    _, _, gains = plan.settle(
        lambda: near,
        far,
        rows,
        (
            [],
            [
                store(
                    "expand",
                    expand_update,
                    gate_summed,
                    up_summed,
                    expand_weight,
                    expand_moment,
                    expand_square,
                )
            ],
            [
                store(
                    "columns",
                    columns_update,
                    shrink_back,
                    mixing_summed,
                    (shrink_weight, shrink_moment, shrink_square),
                    (mixing_weight, mixing_moment, mixing_square),
                )
            ],
        ),
        gains,
        got,
        finish,
    )
    input_gradient = state["input"]
    def order_dp(gains):
        return jnp.take(gains[0], jnp.arange(dp) ^ lax.axis_index("dp"), axis=0)

    gains = step(order_dp, gains)
    for bit in reversed([1 << k for k in range((dp - 1).bit_length())]):
        (got,), _ = window([(gains[bit:], -bit)])
        gains = step(lambda a, b: a[:bit] + b, gains, got)
    gain_grads = gains[0]
    attention_gradient, feedforward_gradient = gain_grads[:1], gain_grads[1:]
    (shrink_gradient, shrink_new), (mixing_gradient, mixing_new) = state["columns"]
    expand_gradient, *expand_new = state["expand"]
    entry_gradient = entry_gradient.astype(F32)
    entry_new = adamw(entry_weight, entry_gradient, entry_moment, entry_square, RATE, DECAY)
    attention_new = adamw(
        attention_gain, attention_gradient, attention_moment, attention_square, GAIN_RATE, 0.0
    )
    feedforward_new = adamw(
        feedforward_gain,
        feedforward_gradient,
        feedforward_moment,
        feedforward_square,
        GAIN_RATE,
        0.0,
    )
    return (
        layer_output,
        input_gradient,
        entry_gradient,
        mixing_gradient,
        attention_gradient,
        expand_gradient,
        shrink_gradient,
        feedforward_gradient,
        entry_new[0],
        mixing_new[0],
        attention_new[0],
        expand_new[0],
        shrink_new[0],
        feedforward_new[0],
        entry_new[1],
        entry_new[2],
        mixing_new[1],
        mixing_new[2],
        attention_new[1],
        attention_new[2],
        expand_new[1],
        expand_new[2],
        shrink_new[1],
        shrink_new[2],
        feedforward_new[1],
        feedforward_new[2],
    )


def solution(mesh):
    placed = (
        P(("dp", "fsdp"), None),
        P(("dp", "fsdp")),
        P(("dp", "fsdp"), None),
        P(None, ("dp", "fsdp"), None),
        P(None, ("dp", "fsdp"), None),
        P(None, ("dp", "fsdp")),
        P(None, ("dp", "fsdp"), None),
        P(None, ("dp", "fsdp"), None),
        P(None, ("dp", "fsdp")),
        P(None, ("dp", "fsdp"), None),
        P(None, ("dp", "fsdp"), None),
        P(None, ("dp", "fsdp"), None),
        P(None, ("dp", "fsdp"), None),
        P(None, ("dp", "fsdp")),
        P(None, ("dp", "fsdp")),
        P(None, ("dp", "fsdp"), None),
        P(None, ("dp", "fsdp"), None),
        P(None, ("dp", "fsdp"), None),
        P(None, ("dp", "fsdp"), None),
        P(None, ("dp", "fsdp")),
        P(None, ("dp", "fsdp")),
    )
    return jax.shard_map(
        functools.partial(local, mesh.shape["dp"], mesh.shape["fsdp"]),
        mesh=mesh,
        in_specs=placed,
        out_specs=(
            P(("dp", "fsdp"), None),
            P(("dp", "fsdp"), None),
            P(None, ("dp", "fsdp"), None),
            P(None, ("dp", "fsdp"), None),
            P(None, ("dp", "fsdp")),
            P(None, ("dp", "fsdp"), None),
            P(None, ("dp", "fsdp"), None),
            P(None, ("dp", "fsdp")),
            P(None, ("dp", "fsdp"), None),
            P(None, ("dp", "fsdp"), None),
            P(None, ("dp", "fsdp")),
            P(None, ("dp", "fsdp"), None),
            P(None, ("dp", "fsdp"), None),
            P(None, ("dp", "fsdp")),
            P(None, ("dp", "fsdp"), None),
            P(None, ("dp", "fsdp"), None),
            P(None, ("dp", "fsdp"), None),
            P(None, ("dp", "fsdp"), None),
            P(None, ("dp", "fsdp")),
            P(None, ("dp", "fsdp")),
            P(None, ("dp", "fsdp"), None),
            P(None, ("dp", "fsdp"), None),
            P(None, ("dp", "fsdp"), None),
            P(None, ("dp", "fsdp"), None),
            P(None, ("dp", "fsdp")),
            P(None, ("dp", "fsdp")),
        ),
        check_vma=False,
    )
```

```python
import functools

import jax
import jax.numpy as jnp
from jax import lax
from jax.experimental import pallas as pl
from jax.experimental.pallas import tpu as pltpu
from jax.sharding import PartitionSpec as P

HEADS = 32
HEAD = 64
STEP = 3


EPS = 1e-05
THETA = 130000.0
RATE = 0.01
MIXING_RATE = 0.04
GAIN_RATE = 0.3
BETA_ONE = 0.9
BETA_TWO = 0.95
ADAM_EPS = 1e-08
DECAY = 0.1


def contract_last(left, right):
    return lax.dot_general(
        left, right, (((1,), (1,)), ((), ())), preferred_element_type=jnp.float32
    )


def contract_first(left, right):
    return lax.dot_general(
        left, right, (((0,), (0,)), ((), ())), preferred_element_type=jnp.float32
    )


def plain_product(left, right):
    return jnp.dot(left, right, preferred_element_type=jnp.float32)


def rope_tables(positions):
    half = HEAD // 2
    freq = THETA ** (-2.0 * jnp.arange(half, dtype=jnp.float32) / HEAD)
    angle = positions.astype(jnp.float32)[:, None] * freq[None, :]
    return (jnp.cos(angle), jnp.sin(angle))


def norm_back(value, scale, gain, grad):
    weighted = grad * gain
    inner = jnp.mean(weighted * value, axis=-1, keepdims=True)
    back = scale * weighted - value * (scale * scale * scale) * inner
    return (back, jnp.sum(grad * value * scale, axis=0))


def adamw(weight, gradient, moment, square, rate, decay):
    moment_new = BETA_ONE * moment + (1.0 - BETA_ONE) * gradient
    square_new = BETA_TWO * square + (1.0 - BETA_TWO) * gradient * gradient
    corrected = moment_new / (1.0 - BETA_ONE**STEP)
    spread = jnp.sqrt(square_new / (1.0 - BETA_TWO**STEP)) + ADAM_EPS
    return (weight - rate * (corrected / spread + decay * weight), moment_new, square_new)


AXES = ("dp", "fsdp")
VMEM_BYTES = 56 * 2**20
BF16 = jnp.bfloat16
F32 = jnp.float32


def add_low(*values):
    return sum(value.astype(F32) for value in values).astype(BF16)


def probs_of(left, right, places_down, places_across, turned):
    rows = right.shape[0]
    down = lax.broadcasted_iota(jnp.int32, (rows, rows), 0)
    across = lax.broadcasted_iota(jnp.int32, (rows, rows), 1)
    earlier = down <= across if turned else across <= down
    visible = (places_down - places_across == down - across) & earlier
    raw = contract_last(left, right).reshape(-1, rows, rows)
    scores = jnp.where(visible[None], raw * (HEAD ** (-0.5)), -1e30)
    axis = 1 if turned else 2
    weights = jnp.exp(scores - jnp.max(scores, axis=axis, keepdims=True))
    return weights * (1.0 / jnp.sum(weights, axis=axis, keepdims=True))


def by_head(value):
    head = lax.broadcasted_iota(jnp.int32, value.shape, 1) // HEAD
    none = jnp.zeros_like(value)
    return jnp.concatenate(
        [jnp.where(head == h, value, none) for h in range(value.shape[1] // HEAD)]
    )


def own_columns(value, rows):
    head = lax.broadcasted_iota(jnp.int32, (rows, value.shape[1]), 1) // HEAD
    total = value[:rows]
    for h in range(1, value.shape[1] // HEAD):
        total = jnp.where(head == h, value[h * rows : (h + 1) * rows], total)
    return total


def swap_halves(value):
    columns = value.shape[1]
    half = HEAD // 2
    lane = lax.broadcasted_iota(jnp.int32, value.shape, 1) % HEAD
    return jnp.where(
        lane < half, pltpu.roll(value, columns - half, 1), pltpu.roll(value, half, 1)
    )


def attend_kernel(group, *refs):
    blocks, refs = refs[:group], refs[group:]
    gain, weight, cosine, sine, down, across, normed, joint, attended, held = refs
    for k in range(group):

        @pl.when(pl.program_id(0) == k)
        def _():
            held[...] = blocks[k][...]

    value = held[...].astype(F32)
    scale = lax.rsqrt(jnp.mean(value * value, axis=-1, keepdims=True) + EPS)
    normed[...] = (value * scale * gain[...]).astype(BF16)
    mixed = contract_last(normed[...], weight[...])
    span = mixed.shape[1] // 3
    for part in range(2):
        piece = mixed[:, part * span : (part + 1) * span]
        joint[:, part * span : (part + 1) * span] = (
            piece * cosine[...] + swap_halves(piece) * sine[...]
        ).astype(BF16)
    joint[:, 2 * span :] = mixed[:, 2 * span :].astype(BF16)
    query, keys, values = (joint[:, part * span : (part + 1) * span] for part in range(3))
    rows = query.shape[0]
    probs = probs_of(by_head(query), keys, down[0, :, :1], across[0, :1], False).astype(BF16)
    found = plain_product(probs.reshape(-1, rows), values)
    attended[...] = own_columns(found, rows).astype(BF16)


def attend_blocks(span, blocks, gain, weight, cosine, sine, down, across):
    group = len(blocks)
    rows, width = blocks[0].shape
    whole = lambda *shape: pl.BlockSpec(shape, lambda i: (0,) * len(shape))
    by_row = lambda columns: pl.BlockSpec((rows, columns), lambda i: (i, 0))
    return pl.pallas_call(
        functools.partial(attend_kernel, group),
        grid=(group,),
        in_specs=[whole(rows, width)] * group
        + [whole(1, width), whole(3 * span, width), by_row(span), by_row(span)]
        + [
            pl.BlockSpec((1, rows, 128), lambda i: (i, 0, 0)),
            pl.BlockSpec((1, 8, rows), lambda i: (i, 0, 0)),
        ],
        out_specs=[by_row(width), by_row(3 * span), by_row(span)],
        out_shape=[
            jax.ShapeDtypeStruct((group * rows, columns), BF16)
            for columns in (width, 3 * span, span)
        ],
        scratch_shapes=[pltpu.VMEM((rows, width), BF16)],
        compiler_params=pltpu.CompilerParams(vmem_limit_bytes=VMEM_BYTES),
    )(*blocks, gain[None], weight, cosine, sine, down, across)


def attend_back_kernel(group, first, *refs):
    grads, blocks, refs = refs[:group], refs[group : 2 * group], refs[2 * group :]
    mixing, weight, joint, attended, normed, cosine, sine, down, across = refs[:9]
    earlier, refs = (None, refs[9:]) if first else (refs[9:12], refs[12:])
    terms, entry_sum, mixing_sum, gain_sum, held, tokens, back, mixing_total = refs
    step = pl.program_id(0)
    for k in range(group):

        @pl.when(step == k)
        def _():
            held[...] = grads[k][...]
            tokens[...] = blocks[k][...]

    @pl.when(step == 0)
    def _():
        for k, sums in ((1, mixing_total), (2, gain_sum)):
            sums[...] = jnp.zeros_like(sums) if first else earlier[k][...]

    rows = held.shape[0]
    here = pl.ds(pl.multiple_of(step * rows, rows), rows)
    span = joint.shape[1] // 3
    query, keys, values = (joint[:, part * span : (part + 1) * span] for part in range(3))
    grad = plain_product(held[...], mixing[...]).astype(BF16)
    key_heads = by_head(keys)
    probs = probs_of(key_heads, query, down[0, :, :1], across[0, :1], True)
    prob_grad = contract_last(by_head(values), grad).reshape(probs.shape)
    delta = jnp.sum(probs * prob_grad, axis=1, keepdims=True)
    score_grad = (probs * (prob_grad - delta)).astype(BF16).reshape(-1, rows)
    query_grad = contract_first(score_grad, key_heads)
    key_grad = own_columns(plain_product(score_grad, query), rows)
    value_grad = own_columns(plain_product(probs.astype(BF16).reshape(-1, rows), grad), rows)
    for part, value in enumerate((query_grad, key_grad)):
        value = value * (HEAD ** (-0.5))
        back[here, part * span : (part + 1) * span] = (
            value * cosine[...] - swap_halves(value) * sine[...]
        ).astype(BF16)
    back[here, 2 * span :] = value_grad.astype(BF16)
    term = plain_product(back[here, :], weight[...])
    terms[...] = term.astype(BF16)
    value = tokens[...].astype(F32)
    scale = lax.rsqrt(jnp.mean(value * value, axis=-1, keepdims=True) + EPS)
    gain_sum[...] += jnp.sum(term * (value * scale), axis=0, keepdims=True)
    mixing_total[...] += contract_first(attended[...], held[...])

    @pl.when(step == group - 1)
    def _():
        for part in range(3):
            part = slice(part * span, (part + 1) * span)
            found = contract_first(back[:, part], normed[...])
            if not first:
                found += earlier[0][part, :]
            entry_sum[part, :] = found.astype(entry_sum.dtype)
        mixing_sum[...] = mixing_total[...].astype(mixing_sum.dtype)


def attend_back_blocks(span, grads, blocks, mixing, weight, joint, attended, normed, turn, earlier):
    group = len(blocks)
    rows, width = blocks[0].shape
    whole = lambda *shape: pl.BlockSpec(shape, lambda i: (0,) * len(shape))
    by_row = lambda columns: pl.BlockSpec((rows, columns), lambda i: (i, 0))
    sums = [(3 * span, width), (span, width), (1, width)]
    return pl.pallas_call(
        functools.partial(attend_back_kernel, group, not earlier),
        grid=(group,),
        in_specs=[whole(rows, width)] * (2 * group)
        + [whole(width, span), whole(3 * span, width)]
        + [by_row(3 * span), by_row(span), whole(group * rows, width), by_row(span), by_row(span)]
        + [
            pl.BlockSpec((1, rows, 128), lambda i: (i, 0, 0)),
            pl.BlockSpec((1, 8, rows), lambda i: (i, 0, 0)),
        ]
        + [whole(*shape) for shape in sums if earlier],
        out_specs=[by_row(width)] + [whole(*shape) for shape in sums],
        out_shape=[jax.ShapeDtypeStruct((group * rows, width), BF16)]
        + [
            jax.ShapeDtypeStruct(shape, BF16 if earlier and shape[0] > 1 else F32) for shape in sums
        ],
        scratch_shapes=[
            pltpu.VMEM((rows, width), BF16),
            pltpu.VMEM((rows, width), BF16),
            pltpu.VMEM((group * rows, 3 * span), BF16),
            pltpu.VMEM((span, width), F32),
        ],
        compiler_params=pltpu.CompilerParams(vmem_limit_bytes=VMEM_BYTES),
    )(
        *grads,
        *blocks,
        mixing,
        weight,
        joint,
        attended,
        normed,
        *turn,
        *earlier,
    )


def turn_tables(places, heads):
    cosine, sine = rope_tables(places.reshape(-1))
    return (
        jnp.tile(jnp.concatenate([cosine, cosine], axis=1), (1, heads)),
        jnp.tile(jnp.concatenate([-sine, sine], axis=1), (1, heads)),
        jnp.broadcast_to(places[:, :, None], (*places.shape, 128)),
        jnp.broadcast_to(places[:, None, :], (places.shape[0], 8, places.shape[1])),
    )


def split_kernel(fsdp, rows_held, blocks):
    width = blocks.shape[2] // HEAD
    for role in range(fsdp):
        for k in range(width):
            first = (k * fsdp + role) * HEAD
            blocks[role, :, k * HEAD : (k + 1) * HEAD] = rows_held[:, first : first + HEAD]


def split_heads(weight, dp, fsdp, span):
    return pl.pallas_call(
        functools.partial(split_kernel, fsdp),
        grid=(1,),
        in_specs=[pl.BlockSpec((span, weight.shape[1]), lambda i: (3, 0))],
        out_specs=pl.BlockSpec((fsdp, span, dp * HEAD), lambda i: (0, 0, 0)),
        out_shape=jax.ShapeDtypeStruct((fsdp, span, dp * HEAD), BF16),
    )(weight)


def expand_kernel(group, *refs):
    blocks, weight, joined, gate, upward, hidden = refs[:group], *refs[group:]
    rows = blocks[0].shape[0]

    @pl.when(pl.program_id(0) == 0)
    def _():
        for k in range(group):
            joined[k * rows : (k + 1) * rows, :] = blocks[k][...]

    gate[...] = contract_last(joined[...], weight[0])
    upward[...] = contract_last(joined[...], weight[1])
    hidden[...] = (gate[...] * jax.nn.sigmoid(gate[...]) * upward[...]).astype(BF16)


def expand_blocks(blocks, weight):
    group = len(blocks)
    rows, width = blocks[0].shape
    units = weight.shape[1]
    tile = min(units, 256)
    by_unit = pl.BlockSpec((group * rows, tile), lambda j: (0, j))
    shape = group * rows, units
    return pl.pallas_call(
        functools.partial(expand_kernel, group),
        grid=(units // tile,),
        in_specs=[pl.BlockSpec((rows, width), lambda j: (0, 0))] * group
        + [pl.BlockSpec((2, tile, width), lambda j: (0, j, 0))],
        out_specs=[pl.BlockSpec((group * rows, width), lambda j: (0, 0))] + [by_unit] * 3,
        out_shape=[
            jax.ShapeDtypeStruct((group * rows, width), BF16),
            jax.ShapeDtypeStruct(shape, F32),
            jax.ShapeDtypeStruct(shape, F32),
            jax.ShapeDtypeStruct(shape, BF16),
        ],
        compiler_params=pltpu.CompilerParams(vmem_limit_bytes=VMEM_BYTES),
    )(*blocks, weight)


def pairs_kernel(left, right, left_other, right_other, out):
    total = contract_first(left[...], right[...])
    total += contract_first(left_other[...], right_other[...])
    out[...] = total.astype(BF16)


def product_pairs(left, right, left_other, right_other):
    rows, units = left.shape
    width = right.shape[1]
    tile = min(units, 256)
    whole = pl.BlockSpec((rows, width), lambda j: (0, 0))
    part = pl.BlockSpec((rows, tile), lambda j: (0, j))
    return pl.pallas_call(
        pairs_kernel,
        grid=(units // tile,),
        in_specs=[part, whole, part, whole],
        out_specs=pl.BlockSpec((tile, width), lambda j: (j, 0)),
        out_shape=jax.ShapeDtypeStruct((units, width), BF16),
        compiler_params=pltpu.CompilerParams(vmem_limit_bytes=VMEM_BYTES),
    )(left, right, left_other, right_other)


def output_kernel(hidden, shrink, head, tail):
    total = contract_last(hidden[...], shrink[...]).astype(BF16)
    head[...] = total[: head.shape[0]]
    tail[...] = total[head.shape[0] :]


def output_blocks(cut, hidden, shrink):
    rows, units = hidden.shape
    width = shrink.shape[0]
    cuts = 4
    return pl.pallas_call(
        output_kernel,
        grid=(cuts,),
        in_specs=[
            pl.BlockSpec((rows, units), lambda j: (0, 0)),
            pl.BlockSpec((width // cuts, units), lambda j: (j, 0)),
        ],
        out_specs=[
            pl.BlockSpec((cut, width // cuts), lambda j: (0, j)),
            pl.BlockSpec((rows - cut, width // cuts), lambda j: (0, j)),
        ],
        out_shape=[
            jax.ShapeDtypeStruct((cut, width), BF16),
            jax.ShapeDtypeStruct((rows - cut, width), BF16),
        ],
        compiler_params=pltpu.CompilerParams(vmem_limit_bytes=VMEM_BYTES),
    )(hidden, shrink)


def expand_back_kernel(tiles, *refs):
    grads, gate, upward, shrink, weight, gate_grad, up_grad, head, tail, both = refs
    step = pl.program_id(0)
    tile = gate.shape[1]

    @pl.when(step < tiles)
    def _():
        sigma = jax.nn.sigmoid(gate[...])
        swish = gate[...] * sigma
        hidden_grad = plain_product(grads[...], shrink[...])
        slope = sigma * (1.0 + gate[...] * (1.0 - sigma))
        gate_grad[...] = (hidden_grad * upward[...] * slope).astype(BF16)
        up_grad[...] = (hidden_grad * swish).astype(BF16)
        both[step] = gate_grad[...]
        both[tiles + step] = up_grad[...]

    @pl.when(step >= tiles)
    def _():
        total = jnp.zeros((grads.shape[0], head.shape[1]), F32)
        for k in range(2 * tiles):
            part, first = k // tiles, k % tiles * tile
            total += plain_product(both[k], weight[part, first : first + tile, :])
        head[...] = total[: head.shape[0]].astype(BF16)
        tail[...] = total[head.shape[0] :].astype(BF16)


def expand_back_blocks(cut, grads, gate, upward, shrink, weight):
    rows, width = grads.shape
    units = gate.shape[1]
    tile = min(units, 256)
    tiles = units // tile
    cuts = 4
    early = lambda j: jnp.minimum(j, tiles - 1)
    late = lambda j: jnp.maximum(j - tiles, 0)
    by_unit = pl.BlockSpec((rows, tile), lambda j: (0, early(j)))
    return pl.pallas_call(
        functools.partial(expand_back_kernel, tiles),
        grid=(tiles + cuts,),
        in_specs=[
            pl.BlockSpec((rows, width), lambda j: (0, 0)),
            by_unit,
            by_unit,
            pl.BlockSpec((width, tile), lambda j: (0, early(j))),
            pl.BlockSpec((2, units, width // cuts), lambda j: (0, 0, late(j))),
        ],
        out_specs=[
            by_unit,
            by_unit,
            pl.BlockSpec((cut, width // cuts), lambda j: (0, late(j))),
            pl.BlockSpec((rows - cut, width // cuts), lambda j: (0, late(j))),
        ],
        out_shape=[
            jax.ShapeDtypeStruct((rows, units), BF16),
            jax.ShapeDtypeStruct((rows, units), BF16),
            jax.ShapeDtypeStruct((cut, width), BF16),
            jax.ShapeDtypeStruct((rows - cut, width), BF16),
        ],
        scratch_shapes=[pltpu.VMEM((2 * tiles, rows, tile), BF16)],
        compiler_params=pltpu.CompilerParams(vmem_limit_bytes=VMEM_BYTES),
    )(grads, gate, upward, shrink, weight)


class Plan:
    def __init__(self, dp, fsdp):
        self.dp, self.fsdp = dp, fsdp
        self.clock = None
        self.bits = [1 << k for k in range(1, (fsdp - 1).bit_length())] + [1]
        self.short = fsdp == 8

    def tie(self, values):
        if self.clock is None:
            return tuple(values)
        return lax.optimization_barrier((tuple(values), self.clock))[0]

    def step(self, work, *values):
        found = work(*self.tie(values))
        self.clock = jax.tree.leaves(found)
        return found

    def window(self, sends, *works):
        values = self.tie([value for value, _ in sends])
        came = []
        for value, (_, mask) in zip(values, sends):
            axis, count = ("fsdp", self.fsdp) if mask > 0 else ("dp", self.dp)
            pairs = [(i, i ^ abs(mask)) for i in range(count)]
            came.append(lax.ppermute(value, axis, pairs))
        gave, done = [], []
        for work in works:
            gave.append(work())
            done += self.clock
        came, self.clock = lax.optimization_barrier((came, done or came))
        return came, gave

    def wait(self, value):
        self.clock = [*self.clock, value]
        return value

    def merge(self, rows, sums, first, second):
        half = rows // 2
        beside, above = sums[rows : 2 * rows], sums[2 * rows : 3 * rows]
        return (
            jnp.concatenate([beside[:half], add_low(beside[half:], second)]),
            jnp.concatenate([add_low(above[:half], first), above[half:]]),
        )

    def spread(self, block, marks=None, works=((), (), ()), extra=None, pause=None):
        small = marks is not None
        gave, more = [], []

        def added(k):
            return [] if extra is None else extra(k, more)

        if self.short:
            half = block.shape[0] // 2
            (beside, above, other, *got), found = self.window(
                [(block, 2), (block, 4), (block, 1)] + [(marks, 2)] * small + added(0), *works[0]
            )
            gave += found
            more.append(got)
            if pause is not None:
                pause()
            if small:
                marks = self.step(lambda a, b: jnp.concatenate([a, b]), marks, *got)
            upper, lower, pair = self.step(
                lambda a, b: (a[:half], b[half:], jnp.concatenate([b, a])), above, beside
            )
            (first, second, pair, *got), found = self.window(
                [(upper, 2), (lower, 4), (pair, 1)] + [(marks, 4)] * small + added(1),
                *[functools.partial(w, [block, beside, above, other]) for w in works[1]],
            )
            gave += found
            more.append(got)
            across = self.step(lambda a, b: jnp.concatenate([a, b]), first, second)
            if small:
                marks = self.step(lambda a, b: jnp.concatenate([a, b]), marks, *got)
            near = [block, beside, above, across]
            (far, *got), found = self.window(
                [(across, 1)] + [(marks, 1)] * small + added(2),
                *[functools.partial(w, near) for w in works[2]],
            )
            more.append(got)
            size = block.shape[0]
            got = got if extra is None else more
            return near, [other, pair[:size], pair[size:], far], (marks, *got), gave + found
        near = [block]
        for bit in self.bits[:-1]:
            got, _ = self.window([(piece, bit) for piece in near] + [(marks, bit)] * small)
            if small:
                marks = jnp.concatenate([marks, got[-1]])
            near = near + got[: len(near)]
        for work in [*works[0], *([pause] if pause else []), *works[1]]:
            gave.append(work())
        got, found = self.window(
            [(piece, 1) for piece in near] + [(marks, 1)] * small,
            *[functools.partial(w, near) for w in works[2]],
        )
        return near, got[: len(near)], (marks, *got[len(near) :]), gave + found

    def settle(self, near, far, rows, works=((), (), ()), small=None, got=None, finish=None):
        gave = []

        def sends(bit):
            return [] if small is None else [(small[bit:], bit)]

        def sum_small(got, bit):
            if got:
                return self.step(lambda a, b: a[:bit] + b, small, *got)
            return None

        if not self.short:
            terms = jnp.concatenate([near(), far])
            for work in [*works[0], *works[1], *works[2]]:
                gave.append(work())
            for bit in reversed(self.bits):
                size = terms.shape[0] // 2
                if got is None:
                    (got,), _ = self.window([(terms[size:], bit)])
                terms = self.step(add_low, terms[:size], got)
                got = None
            if small is not None:
                for bit in sorted(self.bits, reverse=True):
                    small = sum_small(self.window(sends(bit))[0], bit)
            parts = terms, jnp.zeros_like(terms), jnp.zeros_like(terms)
            if finish is not None:
                finish(*parts)
            return parts, gave, small
        half = rows // 2
        if got is None:
            (got,), (near, *found) = self.window([(far, 1)], near, *works[0])
            gave += found
        else:
            near = near()
        sums = self.step(add_low, near, got)
        across = sums[3 * rows :]
        (first, second, *more), found = self.window(
            [(across[:half], 2), (across[half:], 4)] + sends(4), *works[1]
        )
        gave += found
        small = sum_small(more, 4)

        beside, above = self.step(functools.partial(self.merge, rows), sums, first, second)
        (beside, above, *more), found = self.window([(beside, 2), (above, 4)] + sends(2), *works[2])
        small = sum_small(more, 2)
        if small is not None:
            (more,), _ = self.window(sends(1), lambda: finish(sums[:rows], beside, above))
            small = sum_small([more], 1)
        return (sums[:rows], beside, above), gave + found, small

    def sum_pair(self, rows, near, across, got):
        return add_low(near[rows:], got[: 2 * rows]), add_low(across, got[2 * rows :])

    def merge_pair(self, rows, pair, first, second):
        return self.merge(rows, jnp.concatenate([pair[:rows], pair]), first, second)

    def settle_mixed(self, first, across, others, rows, works):
        half = rows // 2
        (got,), ((near, other), *gave) = self.window([(others, 1)], first, *works[0])
        pair, across = self.step(functools.partial(self.sum_pair, rows), near, across, got)
        (upper, lower, own), found = self.window(
            [(across[:half], 2), (across[half:], 4), (other, 1)], *works[1]
        )
        gave += found
        beside, above = self.step(functools.partial(self.merge_pair, rows), pair, upper, lower)
        (beside, above), found = self.window([(beside, 2), (above, 4)], *works[2])
        return (near[:rows], own, beside, above), gave + found

    def columns_split(self, shard):
        rows, columns = shard.shape
        width = columns // (self.dp * self.fsdp)
        blocks = shard.reshape(rows, self.dp, self.fsdp, width).transpose(2, 0, 1, 3)
        return blocks.reshape(self.fsdp, rows, self.dp * width)

    def exchange(self, blocks):
        return lax.all_to_all(blocks, "fsdp", 0, 0, tiled=True)

    def columns_back(self, *sums):
        rows = sums[0].shape[0] // self.fsdp
        blocks = [value.reshape(self.fsdp, rows, -1) for value in sums]
        blocks = self.exchange(jnp.concatenate(blocks, axis=-1))
        found, last = [], 0
        for value in sums:
            first, last = last, last + value.shape[1]
            block = blocks[..., first:last].reshape(self.fsdp, rows, self.dp, -1)
            found.append(block.transpose(1, 2, 0, 3).reshape(rows, self.fsdp * value.shape[1]))
        return found


def local(
    dp,
    fsdp,
    tokens,
    positions,
    cotangent,
    entry_weight,
    mixing_weight,
    attention_gain,
    expand_weight,
    shrink_weight,
    feedforward_gain,
    entry_moment,
    entry_square,
    mixing_moment,
    mixing_square,
    attention_moment,
    attention_square,
    expand_moment,
    expand_square,
    shrink_moment,
    shrink_square,
    feedforward_moment,
    feedforward_square,
):
    plan = Plan(dp, fsdp)
    step, window, wait = plan.step, plan.window, plan.wait
    rows = tokens.shape[0]
    width = tokens.shape[1]
    group = fsdp // 2
    whole_heads = entry_weight.shape[1] == HEAD
    heads = HEADS // fsdp
    span = heads * HEAD
    factor = HEAD ** (-0.5)
    state = {}

    def work(call, *values):
        return lambda *_: step(call, *values)

    def store(name, call, *values):
        def run(*_):
            state[name] = step(call, *values)

        return run

    def low_of(value):
        return value.astype(BF16)

    join = lambda *a: jnp.concatenate(a)
    product_last = lambda a, b: contract_last(a, b).astype(BF16)
    product_plain = lambda a, b: plain_product(a, b).astype(BF16)

    attention_low = step(
        lambda a, b: jnp.concatenate([a, b]).astype(BF16), entry_weight, mixing_weight
    )
    role = lax.axis_index("fsdp")
    if whole_heads:
        attention_all = lax.all_gather(attention_low, "dp", axis=1, tiled=True)
    else:
        attention_all = lax.all_gather(attention_low, AXES, axis=1, tiled=True)

    def gains_dp(*gains):
        gains = jnp.concatenate(gains).astype(BF16)[:, None]
        return lax.all_gather(gains, "dp", axis=1, tiled=True)

    def gains_fsdp(gains):
        return lax.all_gather(gains[:, :, None], "fsdp", axis=2, tiled=True)

    def columns_work(rows_held):
        return plan.exchange(plan.columns_split(rows_held))

    spread_tokens, far_tokens, (near_places, far_places), _ = plan.spread(
        tokens,
        positions[None],
        (
            [
                store("gains_dp", gains_dp, attention_gain, feedforward_gain),
                store("expand_low", low_of, expand_weight),
            ],
            [lambda *_: state.update(gains=step(gains_fsdp, state["gains_dp"]))],
            [],
        ),
    )
    gains = state["gains"].reshape(2, width).astype(F32)
    gain_one, gain_two = gains[0], gains[1]
    expand_role = lax.all_gather(state["expand_low"], "dp", axis=1, tiled=True)

    inputs = tokens.astype(F32)
    live = (positions >= 0).astype(F32)[:, None]
    grad_out = cotangent.astype(F32) * live
    grad_low = step(low_of, grad_out)
    state["turn near"] = step(lambda a: turn_tables(a, heads), near_places)
    state["turn far"] = step(lambda a: turn_tables(a, heads), far_places)

    def attend_work(name, blocks):
        def run(*_):
            state["attend " + name] = step(
                functools.partial(attend_blocks, span),
                blocks,
                gain_one,
                state["entry"],
                *state["turn " + name],
            )

        return run

    def attention_weights():
        found = wait(attention_all)
        if whole_heads:
            state["entry"] = found.reshape(4 * span, width)
            (held,) = plan.tie([split_heads(state["entry"], dp, fsdp, span)])
            mixing_role = plan.exchange(held).reshape(fsdp, dp, HEAD, span)
            state["mixing"] = mixing_role.transpose(1, 0, 2, 3).reshape(width, span)
        else:
            own = lax.dynamic_slice_in_dim(found[:3], role * span, span, axis=1)
            state["entry"] = own.reshape(3 * span, width)
            state["mixing"] = lax.dynamic_slice_in_dim(found[3], role * span, span, axis=1)
        attend_work("far", far_tokens)()

    near_grad, far_grad, _, _ = plan.spread(
        grad_low,
        None,
        ([], [attend_work("near", spread_tokens)], []),
        pause=attention_weights,
    )
    mixing_role = wait(state["mixing"])
    entry_role = state["entry"]
    far = step(product_last, state["attend far"][2], mixing_role)
    near = work(product_last, state["attend near"][2], mixing_role)
    shrink_low = step(low_of, shrink_weight[0])
    parts, (shrink_blocks, *_), _ = plan.settle(
        near,
        far,
        rows,
        (
            [work(columns_work, shrink_low)],
            [],
            [],
        ),
    )
    shrink_role = lax.all_gather(shrink_blocks, "dp", axis=0, tiled=True).reshape(width, -1)

    def norm_middle(inputs, gain, own, beside, above):
        middle = inputs + own.astype(F32) + beside.astype(F32) + above.astype(F32)
        scale = lax.rsqrt(jnp.mean(middle * middle, axis=-1, keepdims=True) + EPS)
        return (middle * scale * gain).astype(BF16), middle, scale

    expand_role = wait(expand_role)
    low_two, middle, scale_two = step(norm_middle, inputs, gain_two, *parts)

    def grouped(near, far):
        if not plan.short:
            return near, far
        return [*near[:3], far[0]], [near[3], *far[1:]]

    first_grad, second_grad = grouped(near_grad, far_grad)

    def expand_first(blocks):
        state["up first"] = step(expand_blocks, blocks, expand_role)

    near_two, far_two, _, _ = plan.spread(
        low_two,
        None,
        (
            [store("grad first", join, *first_grad), store("grad second", join, *second_grad)],
            [expand_first] * plan.short,
            [expand_first] * (not plan.short),
        ),
    )
    state["up second"] = step(expand_blocks, grouped(near_two, far_two)[1], expand_role)
    shrink_grad = step(
        product_pairs,
        state["grad first"],
        state["up first"][3],
        state["grad second"],
        state["up second"][3],
    )
    shrink_summed = lax.psum_scatter(shrink_grad, "dp", scatter_dimension=0, tiled=True)
    shrink_role = wait(shrink_role)

    def expand_back(name, cut):
        return step(
            functools.partial(expand_back_blocks, cut * rows),
            state["grad " + name],
            *state["up " + name][1:3],
            shrink_role,
            expand_role,
        )

    second_back = expand_back("second", 1)

    def first_terms():
        state["back"] = expand_back("first", 3)
        return state["back"][2:]

    def expand_grad(index):
        return lambda *_: step(
            product_pairs,
            state["back"][index],
            state["up first"][0],
            second_back[index],
            state["up second"][0],
        )

    works = ([], [expand_grad(0)], [expand_grad(1)])
    if plan.short:
        parts, gave = plan.settle_mixed(first_terms, *second_back[2:], rows, works)
    else:
        parts, gave, _ = plan.settle(
            lambda: join(*first_terms()), join(*second_back[2:]), rows, works
        )
    gate_grad, up_grad = gave

    def output_work(name, cut):
        return store(
            "out " + name,
            functools.partial(output_blocks, cut * rows),
            state["up " + name][3],
            shrink_role,
        )

    gate_summed = lax.psum_scatter(gate_grad, "dp", scatter_dimension=0, tiled=True)
    up_summed = lax.psum_scatter(up_grad, "dp", scatter_dimension=0, tiled=True)

    shrink_summed = wait(shrink_summed)

    def expand_update(gate, up, weight, moment, square):
        gradient = jnp.stack([gate, up]).astype(F32)
        return gradient, *adamw(weight, gradient, moment, square, RATE, DECAY)

    def back_two(middle, scale, gain, grad_out, *parts):
        grad = sum(value.astype(F32) for value in parts)
        middle_back, gain_grad = norm_back(middle, scale, gain, grad)
        middle_grad = grad_out + middle_back
        return middle_grad.astype(BF16), middle_grad, gain_grad

    branch_low, middle_grad, gain_two_grad = step(
        back_two, middle, scale_two, gain_two, grad_out, *parts
    )

    def attend_back(name, grads, blocks, earlier):
        normed, joint, attended = state["attend " + name]
        return step(
            functools.partial(attend_back_blocks, span),
            grads,
            blocks,
            mixing_role,
            entry_role,
            joint,
            attended,
            normed,
            state["turn " + name],
            earlier,
        )

    def order_gains(gain_one_grad, gain_two_grad):
        gains = jnp.stack([gain_one_grad[0], gain_two_grad])
        gains = gains.reshape(2, dp, fsdp, width // (dp * fsdp)).transpose(2, 1, 0, 3)
        return jnp.take(gains, jnp.arange(fsdp) ^ role, axis=0)

    def extra_output(k, came):
        if k == 0:
            return []
        if k == 1:
            return [(state["out second"][1], 1), (state["out first"][1], 1)]
        state["sums"] = step(
            functools.partial(plan.sum_pair, rows),
            state["out first"][0],
            state["out second"][0],
            came[1][0],
        )
        across = state["sums"][1]
        return [(across[: rows // 2], 2), (across[rows // 2 :], 4)]

    def back_near(near_branch):
        state["near back"] = attend_back("near", near_branch, spread_tokens, [])

    def back_far():
        state["far back"] = attend_back(
            "far", far_branch, far_tokens, state["near back"][1:]
        )

    _, far_branch, came, _ = plan.spread(
        branch_low,
        None,
        (
            [output_work("second", 1), output_work("first", 3)],
            [],
            [back_near],
        ),
        extra_output,
    )
    if plan.short:
        beside, above = step(
            functools.partial(plan.merge_pair, rows), state["sums"][0], *came[3]
        )
        parts, _ = window([(beside, 2), (above, 4)], back_far)
        parts = [state["out first"][0][:rows], came[2][1], *parts]
    else:
        parts, _, _ = plan.settle(
            lambda: join(*state["out first"]),
            join(*state["out second"]),
            rows,
            ([], [back_far], []),
        )
    layer_output = step(
        lambda *a: sum((value.astype(F32) for value in a[1:]), a[0]).astype(BF16), middle, *parts
    )
    near, far = state["near back"][0], state["far back"][0]
    gate_summed = wait(gate_summed)
    up_summed = wait(up_summed)

    _, entry_grad, mixing_grad, gain_grad = state["far back"]
    mixing_grad = step(lambda a: a.T, mixing_grad)
    if whole_heads:
        mixing_summed = lax.psum_scatter(mixing_grad, "dp", scatter_dimension=0, tiled=True)
        entry_gradient = lax.psum_scatter(
            entry_grad.reshape(3, dp * HEAD, width), "dp", scatter_dimension=1, tiled=True
        )
    else:
        entry_full = lax.dynamic_update_slice_in_dim(
            jnp.zeros((3, width, width), BF16),
            entry_grad.reshape(3, span, width),
            role * span,
            axis=1,
        )
        mixing_full = lax.dynamic_update_slice_in_dim(
            jnp.zeros((width, width), BF16), mixing_grad, role * span, axis=1
        )
        entry_gradient = lax.psum_scatter(entry_full, AXES, scatter_dimension=1, tiled=True)
        mixing_summed = lax.psum_scatter(mixing_full, AXES, scatter_dimension=0, tiled=True)

    gains = step(order_gains, gain_grad, gain_two_grad)
    (got,), ((shrink_back,),) = window([(far, 1)], work(plan.columns_back, shrink_summed))

    def back_input(inputs, gain, middle_grad, *parts):
        scale = lax.rsqrt(jnp.mean(inputs * inputs, axis=-1, keepdims=True) + EPS)
        grad = sum(value.astype(F32) for value in parts)
        return middle_grad + norm_back(inputs, scale, gain, grad)[0]

    def finish(*parts):
        state["input"] = step(back_input, inputs, gain_one, middle_grad, *parts)

    def columns_update(shrink_back, mixing_summed, shrink, mixing):
        if whole_heads:
            (mixing_summed,) = plan.columns_back(mixing_summed)
        found = []
        for gradient, values, rate in (
            (shrink_back, shrink, RATE),
            (mixing_summed, mixing, MIXING_RATE),
        ):
            gradient = gradient[None].astype(F32)
            found.append((gradient, adamw(values[0], gradient, *values[1:], rate, DECAY)))
        return found

    _, _, gains = plan.settle(
        lambda: near,
        far,
        rows,
        (
            [],
            [
                store(
                    "expand",
                    expand_update,
                    gate_summed,
                    up_summed,
                    expand_weight,
                    expand_moment,
                    expand_square,
                )
            ],
            [
                store(
                    "columns",
                    columns_update,
                    shrink_back,
                    mixing_summed,
                    (shrink_weight, shrink_moment, shrink_square),
                    (mixing_weight, mixing_moment, mixing_square),
                )
            ],
        ),
        gains,
        got,
        finish,
    )
    input_gradient = state["input"]
    def order_dp(gains):
        return jnp.take(gains[0], jnp.arange(dp) ^ lax.axis_index("dp"), axis=0)

    gains = step(order_dp, gains)
    for bit in reversed([1 << k for k in range((dp - 1).bit_length())]):
        (got,), _ = window([(gains[bit:], -bit)])
        gains = step(lambda a, b: a[:bit] + b, gains, got)
    gain_grads = gains[0]
    attention_gradient, feedforward_gradient = gain_grads[:1], gain_grads[1:]
    (shrink_gradient, shrink_new), (mixing_gradient, mixing_new) = state["columns"]
    expand_gradient, *expand_new = state["expand"]
    entry_gradient = entry_gradient.astype(F32)
    entry_new = adamw(entry_weight, entry_gradient, entry_moment, entry_square, RATE, DECAY)
    attention_new = adamw(
        attention_gain, attention_gradient, attention_moment, attention_square, GAIN_RATE, 0.0
    )
    feedforward_new = adamw(
        feedforward_gain,
        feedforward_gradient,
        feedforward_moment,
        feedforward_square,
        GAIN_RATE,
        0.0,
    )
    return (
        layer_output,
        input_gradient,
        entry_gradient,
        mixing_gradient,
        attention_gradient,
        expand_gradient,
        shrink_gradient,
        feedforward_gradient,
        entry_new[0],
        mixing_new[0],
        attention_new[0],
        expand_new[0],
        shrink_new[0],
        feedforward_new[0],
        entry_new[1],
        entry_new[2],
        mixing_new[1],
        mixing_new[2],
        attention_new[1],
        attention_new[2],
        expand_new[1],
        expand_new[2],
        shrink_new[1],
        shrink_new[2],
        feedforward_new[1],
        feedforward_new[2],
    )


def solution(mesh):
    placed = (
        P(("dp", "fsdp"), None),
        P(("dp", "fsdp")),
        P(("dp", "fsdp"), None),
        P(None, ("dp", "fsdp"), None),
        P(None, ("dp", "fsdp"), None),
        P(None, ("dp", "fsdp")),
        P(None, ("dp", "fsdp"), None),
        P(None, ("dp", "fsdp"), None),
        P(None, ("dp", "fsdp")),
        P(None, ("dp", "fsdp"), None),
        P(None, ("dp", "fsdp"), None),
        P(None, ("dp", "fsdp"), None),
        P(None, ("dp", "fsdp"), None),
        P(None, ("dp", "fsdp")),
        P(None, ("dp", "fsdp")),
        P(None, ("dp", "fsdp"), None),
        P(None, ("dp", "fsdp"), None),
        P(None, ("dp", "fsdp"), None),
        P(None, ("dp", "fsdp"), None),
        P(None, ("dp", "fsdp")),
        P(None, ("dp", "fsdp")),
    )
    return jax.shard_map(
        functools.partial(local, mesh.shape["dp"], mesh.shape["fsdp"]),
        mesh=mesh,
        in_specs=placed,
        out_specs=(
            P(("dp", "fsdp"), None),
            P(("dp", "fsdp"), None),
            P(None, ("dp", "fsdp"), None),
            P(None, ("dp", "fsdp"), None),
            P(None, ("dp", "fsdp")),
            P(None, ("dp", "fsdp"), None),
            P(None, ("dp", "fsdp"), None),
            P(None, ("dp", "fsdp")),
            P(None, ("dp", "fsdp"), None),
            P(None, ("dp", "fsdp"), None),
            P(None, ("dp", "fsdp")),
            P(None, ("dp", "fsdp"), None),
            P(None, ("dp", "fsdp"), None),
            P(None, ("dp", "fsdp")),
            P(None, ("dp", "fsdp"), None),
            P(None, ("dp", "fsdp"), None),
            P(None, ("dp", "fsdp"), None),
            P(None, ("dp", "fsdp"), None),
            P(None, ("dp", "fsdp")),
            P(None, ("dp", "fsdp")),
            P(None, ("dp", "fsdp"), None),
            P(None, ("dp", "fsdp"), None),
            P(None, ("dp", "fsdp"), None),
            P(None, ("dp", "fsdp"), None),
            P(None, ("dp", "fsdp")),
            P(None, ("dp", "fsdp")),
        ),
        check_vma=False,
    )
```

```python
import functools

import jax
import jax.numpy as jnp
from jax import lax
from jax.experimental import pallas as pl
from jax.experimental.pallas import tpu as pltpu
from jax.sharding import PartitionSpec as P

HEADS = 32
HEAD = 64
STEP = 3


EPS = 1e-05
THETA = 130000.0
RATE = 0.01
MIXING_RATE = 0.04
GAIN_RATE = 0.3
BETA_ONE = 0.9
BETA_TWO = 0.95
ADAM_EPS = 1e-08
DECAY = 0.1


def contract_last(left, right):
    return lax.dot_general(
        left, right, (((1,), (1,)), ((), ())), preferred_element_type=jnp.float32
    )


def contract_first(left, right):
    return lax.dot_general(
        left, right, (((0,), (0,)), ((), ())), preferred_element_type=jnp.float32
    )


def plain_product(left, right):
    return jnp.dot(left, right, preferred_element_type=jnp.float32)


def rope_tables(positions):
    half = HEAD // 2
    freq = THETA ** (-2.0 * jnp.arange(half, dtype=jnp.float32) / HEAD)
    angle = positions.astype(jnp.float32)[:, None] * freq[None, :]
    return (jnp.cos(angle), jnp.sin(angle))


def norm_back(value, scale, gain, grad):
    weighted = grad * gain
    inner = jnp.mean(weighted * value, axis=-1, keepdims=True)
    back = scale * weighted - value * (scale * scale * scale) * inner
    return (back, jnp.sum(grad * value * scale, axis=0))


def adamw(weight, gradient, moment, square, rate, decay):
    moment_new = BETA_ONE * moment + (1.0 - BETA_ONE) * gradient
    square_new = BETA_TWO * square + (1.0 - BETA_TWO) * gradient * gradient
    corrected = moment_new / (1.0 - BETA_ONE**STEP)
    spread = jnp.sqrt(square_new / (1.0 - BETA_TWO**STEP)) + ADAM_EPS
    return (weight - rate * (corrected / spread + decay * weight), moment_new, square_new)


AXES = ("dp", "fsdp")
VMEM_BYTES = 56 * 2**20
BF16 = jnp.bfloat16
F32 = jnp.float32


def add_low(*values):
    return sum(value.astype(F32) for value in values).astype(BF16)


def probs_of(left, right, places_down, places_across, turned):
    rows = right.shape[0]
    down = lax.broadcasted_iota(jnp.int32, (rows, rows), 0)
    across = lax.broadcasted_iota(jnp.int32, (rows, rows), 1)
    earlier = down <= across if turned else across <= down
    visible = (places_down - places_across == down - across) & earlier
    raw = contract_last(left, right).reshape(-1, rows, rows)
    scores = jnp.where(visible[None], raw * (HEAD ** (-0.5)), -1e30)
    axis = 1 if turned else 2
    weights = jnp.exp(scores - jnp.max(scores, axis=axis, keepdims=True))
    return weights * (1.0 / jnp.sum(weights, axis=axis, keepdims=True))


def by_head(value):
    head = lax.broadcasted_iota(jnp.int32, value.shape, 1) // HEAD
    none = jnp.zeros_like(value)
    return jnp.concatenate(
        [jnp.where(head == h, value, none) for h in range(value.shape[1] // HEAD)]
    )


def own_columns(value, rows):
    head = lax.broadcasted_iota(jnp.int32, (rows, value.shape[1]), 1) // HEAD
    total = value[:rows]
    for h in range(1, value.shape[1] // HEAD):
        total = jnp.where(head == h, value[h * rows : (h + 1) * rows], total)
    return total


def swap_halves(value):
    columns = value.shape[1]
    half = HEAD // 2
    lane = lax.broadcasted_iota(jnp.int32, value.shape, 1) % HEAD
    return jnp.where(
        lane < half, pltpu.roll(value, columns - half, 1), pltpu.roll(value, half, 1)
    )


def attend_kernel(group, *refs):
    blocks, refs = refs[:group], refs[group:]
    gain, weight, cosine, sine, down, across, normed, joint, attended, held = refs
    for k in range(group):

        @pl.when(pl.program_id(0) == k)
        def _():
            held[...] = blocks[k][...]

    value = held[...].astype(F32)
    scale = lax.rsqrt(jnp.mean(value * value, axis=-1, keepdims=True) + EPS)
    normed[...] = (value * scale * gain[...]).astype(BF16)
    mixed = contract_last(normed[...], weight[...])
    span = mixed.shape[1] // 3
    for part in range(2):
        piece = mixed[:, part * span : (part + 1) * span]
        joint[:, part * span : (part + 1) * span] = (
            piece * cosine[...] + swap_halves(piece) * sine[...]
        ).astype(BF16)
    joint[:, 2 * span :] = mixed[:, 2 * span :].astype(BF16)
    query, keys, values = (joint[:, part * span : (part + 1) * span] for part in range(3))
    rows = query.shape[0]
    probs = probs_of(by_head(query), keys, down[0, :, :1], across[0, :1], False).astype(BF16)
    found = plain_product(probs.reshape(-1, rows), values)
    attended[...] = own_columns(found, rows).astype(BF16)


def attend_blocks(span, blocks, gain, weight, cosine, sine, down, across):
    group = len(blocks)
    rows, width = blocks[0].shape
    whole = lambda *shape: pl.BlockSpec(shape, lambda i: (0,) * len(shape))
    by_row = lambda columns: pl.BlockSpec((rows, columns), lambda i: (i, 0))
    return pl.pallas_call(
        functools.partial(attend_kernel, group),
        grid=(group,),
        in_specs=[whole(rows, width)] * group
        + [whole(1, width), whole(3 * span, width), by_row(span), by_row(span)]
        + [
            pl.BlockSpec((1, rows, 128), lambda i: (i, 0, 0)),
            pl.BlockSpec((1, 8, rows), lambda i: (i, 0, 0)),
        ],
        out_specs=[by_row(width), by_row(3 * span), by_row(span)],
        out_shape=[
            jax.ShapeDtypeStruct((group * rows, columns), BF16)
            for columns in (width, 3 * span, span)
        ],
        scratch_shapes=[pltpu.VMEM((rows, width), BF16)],
        compiler_params=pltpu.CompilerParams(vmem_limit_bytes=VMEM_BYTES),
    )(*blocks, gain[None], weight, cosine, sine, down, across)


def attend_back_kernel(group, first, *refs):
    grads, blocks, refs = refs[:group], refs[group : 2 * group], refs[2 * group :]
    mixing, weight, joint, attended, normed, cosine, sine, down, across = refs[:9]
    earlier, refs = (None, refs[9:]) if first else (refs[9:12], refs[12:])
    terms, entry_sum, mixing_sum, gain_sum, held, tokens, back, mixing_total = refs
    step = pl.program_id(0)
    for k in range(group):

        @pl.when(step == k)
        def _():
            held[...] = grads[k][...]
            tokens[...] = blocks[k][...]

    @pl.when(step == 0)
    def _():
        for k, sums in ((1, mixing_total), (2, gain_sum)):
            sums[...] = jnp.zeros_like(sums) if first else earlier[k][...]

    rows = held.shape[0]
    here = pl.ds(pl.multiple_of(step * rows, rows), rows)
    span = joint.shape[1] // 3
    query, keys, values = (joint[:, part * span : (part + 1) * span] for part in range(3))
    grad = plain_product(held[...], mixing[...]).astype(BF16)
    key_heads = by_head(keys)
    probs = probs_of(key_heads, query, down[0, :, :1], across[0, :1], True)
    prob_grad = contract_last(by_head(values), grad).reshape(probs.shape)
    delta = jnp.sum(probs * prob_grad, axis=1, keepdims=True)
    score_grad = (probs * (prob_grad - delta)).astype(BF16).reshape(-1, rows)
    query_grad = contract_first(score_grad, key_heads)
    key_grad = own_columns(plain_product(score_grad, query), rows)
    value_grad = own_columns(plain_product(probs.astype(BF16).reshape(-1, rows), grad), rows)
    for part, value in enumerate((query_grad, key_grad)):
        value = value * (HEAD ** (-0.5))
        back[here, part * span : (part + 1) * span] = (
            value * cosine[...] - swap_halves(value) * sine[...]
        ).astype(BF16)
    back[here, 2 * span :] = value_grad.astype(BF16)
    term = plain_product(back[here, :], weight[...])
    terms[...] = term.astype(BF16)
    value = tokens[...].astype(F32)
    scale = lax.rsqrt(jnp.mean(value * value, axis=-1, keepdims=True) + EPS)
    gain_sum[...] += jnp.sum(term * (value * scale), axis=0, keepdims=True)
    mixing_total[...] += contract_first(attended[...], held[...])

    @pl.when(step == group - 1)
    def _():
        for part in range(3):
            part = slice(part * span, (part + 1) * span)
            found = contract_first(back[:, part], normed[...])
            if not first:
                found += earlier[0][part, :]
            entry_sum[part, :] = found.astype(entry_sum.dtype)
        mixing_sum[...] = mixing_total[...].astype(mixing_sum.dtype)


def attend_back_blocks(span, grads, blocks, mixing, weight, joint, attended, normed, turn, earlier):
    group = len(blocks)
    rows, width = blocks[0].shape
    whole = lambda *shape: pl.BlockSpec(shape, lambda i: (0,) * len(shape))
    by_row = lambda columns: pl.BlockSpec((rows, columns), lambda i: (i, 0))
    sums = [(3 * span, width), (span, width), (1, width)]
    return pl.pallas_call(
        functools.partial(attend_back_kernel, group, not earlier),
        grid=(group,),
        in_specs=[whole(rows, width)] * (2 * group)
        + [whole(width, span), whole(3 * span, width)]
        + [by_row(3 * span), by_row(span), whole(group * rows, width), by_row(span), by_row(span)]
        + [
            pl.BlockSpec((1, rows, 128), lambda i: (i, 0, 0)),
            pl.BlockSpec((1, 8, rows), lambda i: (i, 0, 0)),
        ]
        + [whole(*shape) for shape in sums if earlier],
        out_specs=[by_row(width)] + [whole(*shape) for shape in sums],
        out_shape=[jax.ShapeDtypeStruct((group * rows, width), BF16)]
        + [
            jax.ShapeDtypeStruct(shape, BF16 if earlier and shape[0] > 1 else F32) for shape in sums
        ],
        scratch_shapes=[
            pltpu.VMEM((rows, width), BF16),
            pltpu.VMEM((rows, width), BF16),
            pltpu.VMEM((group * rows, 3 * span), BF16),
            pltpu.VMEM((span, width), F32),
        ],
        compiler_params=pltpu.CompilerParams(vmem_limit_bytes=VMEM_BYTES),
    )(
        *grads,
        *blocks,
        mixing,
        weight,
        joint,
        attended,
        normed,
        *turn,
        *earlier,
    )


def turn_tables(places, heads):
    cosine, sine = rope_tables(places.reshape(-1))
    return (
        jnp.tile(jnp.concatenate([cosine, cosine], axis=1), (1, heads)),
        jnp.tile(jnp.concatenate([-sine, sine], axis=1), (1, heads)),
        jnp.broadcast_to(places[:, :, None], (*places.shape, 128)),
        jnp.broadcast_to(places[:, None, :], (places.shape[0], 8, places.shape[1])),
    )


def split_kernel(fsdp, rows_held, blocks):
    width = blocks.shape[2] // HEAD
    for role in range(fsdp):
        for k in range(width):
            first = (k * fsdp + role) * HEAD
            blocks[role, :, k * HEAD : (k + 1) * HEAD] = rows_held[:, first : first + HEAD]


def split_heads(weight, dp, fsdp, span):
    return pl.pallas_call(
        functools.partial(split_kernel, fsdp),
        grid=(1,),
        in_specs=[pl.BlockSpec((span, weight.shape[1]), lambda i: (3, 0))],
        out_specs=pl.BlockSpec((fsdp, span, dp * HEAD), lambda i: (0, 0, 0)),
        out_shape=jax.ShapeDtypeStruct((fsdp, span, dp * HEAD), BF16),
    )(weight)


def expand_kernel(group, *refs):
    blocks, weight, joined, gate, upward, hidden = refs[:group], *refs[group:]
    rows = blocks[0].shape[0]

    @pl.when(pl.program_id(0) == 0)
    def _():
        for k in range(group):
            joined[k * rows : (k + 1) * rows, :] = blocks[k][...]

    gate[...] = contract_last(joined[...], weight[0])
    upward[...] = contract_last(joined[...], weight[1])
    hidden[...] = (gate[...] * jax.nn.sigmoid(gate[...]) * upward[...]).astype(BF16)


def expand_blocks(blocks, weight):
    group = len(blocks)
    rows, width = blocks[0].shape
    units = weight.shape[1]
    tile = min(units, 256)
    by_unit = pl.BlockSpec((group * rows, tile), lambda j: (0, j))
    shape = group * rows, units
    return pl.pallas_call(
        functools.partial(expand_kernel, group),
        grid=(units // tile,),
        in_specs=[pl.BlockSpec((rows, width), lambda j: (0, 0))] * group
        + [pl.BlockSpec((2, tile, width), lambda j: (0, j, 0))],
        out_specs=[pl.BlockSpec((group * rows, width), lambda j: (0, 0))] + [by_unit] * 3,
        out_shape=[
            jax.ShapeDtypeStruct((group * rows, width), BF16),
            jax.ShapeDtypeStruct(shape, F32),
            jax.ShapeDtypeStruct(shape, F32),
            jax.ShapeDtypeStruct(shape, BF16),
        ],
        compiler_params=pltpu.CompilerParams(vmem_limit_bytes=VMEM_BYTES),
    )(*blocks, weight)


def pairs_kernel(left, right, left_other, right_other, out):
    total = contract_first(left[...], right[...])
    total += contract_first(left_other[...], right_other[...])
    out[...] = total.astype(BF16)


def product_pairs(left, right, left_other, right_other):
    rows, units = left.shape
    width = right.shape[1]
    tile = min(units, 256)
    whole = pl.BlockSpec((rows, width), lambda j: (0, 0))
    part = pl.BlockSpec((rows, tile), lambda j: (0, j))
    return pl.pallas_call(
        pairs_kernel,
        grid=(units // tile,),
        in_specs=[part, whole, part, whole],
        out_specs=pl.BlockSpec((tile, width), lambda j: (j, 0)),
        out_shape=jax.ShapeDtypeStruct((units, width), BF16),
        compiler_params=pltpu.CompilerParams(vmem_limit_bytes=VMEM_BYTES),
    )(left, right, left_other, right_other)


def output_kernel(hidden, shrink, head, tail):
    total = contract_last(hidden[...], shrink[...]).astype(BF16)
    head[...] = total[: head.shape[0]]
    tail[...] = total[head.shape[0] :]


def output_blocks(cut, hidden, shrink):
    rows, units = hidden.shape
    width = shrink.shape[0]
    cuts = 4
    return pl.pallas_call(
        output_kernel,
        grid=(cuts,),
        in_specs=[
            pl.BlockSpec((rows, units), lambda j: (0, 0)),
            pl.BlockSpec((width // cuts, units), lambda j: (j, 0)),
        ],
        out_specs=[
            pl.BlockSpec((cut, width // cuts), lambda j: (0, j)),
            pl.BlockSpec((rows - cut, width // cuts), lambda j: (0, j)),
        ],
        out_shape=[
            jax.ShapeDtypeStruct((cut, width), BF16),
            jax.ShapeDtypeStruct((rows - cut, width), BF16),
        ],
        compiler_params=pltpu.CompilerParams(vmem_limit_bytes=VMEM_BYTES),
    )(hidden, shrink)


def expand_back_kernel(tiles, *refs):
    grads, gate, upward, shrink, weight, gate_grad, up_grad, head, tail, both = refs
    step = pl.program_id(0)
    tile = gate.shape[1]

    @pl.when(step < tiles)
    def _():
        sigma = jax.nn.sigmoid(gate[...])
        swish = gate[...] * sigma
        hidden_grad = plain_product(grads[...], shrink[...])
        slope = sigma * (1.0 + gate[...] * (1.0 - sigma))
        gate_grad[...] = (hidden_grad * upward[...] * slope).astype(BF16)
        up_grad[...] = (hidden_grad * swish).astype(BF16)
        both[step] = gate_grad[...]
        both[tiles + step] = up_grad[...]

    @pl.when(step >= tiles)
    def _():
        total = jnp.zeros((grads.shape[0], head.shape[1]), F32)
        for k in range(2 * tiles):
            part, first = k // tiles, k % tiles * tile
            total += plain_product(both[k], weight[part, first : first + tile, :])
        head[...] = total[: head.shape[0]].astype(BF16)
        tail[...] = total[head.shape[0] :].astype(BF16)


def expand_back_blocks(cut, grads, gate, upward, shrink, weight):
    rows, width = grads.shape
    units = gate.shape[1]
    tile = min(units, 256)
    tiles = units // tile
    cuts = 4
    early = lambda j: jnp.minimum(j, tiles - 1)
    late = lambda j: jnp.maximum(j - tiles, 0)
    by_unit = pl.BlockSpec((rows, tile), lambda j: (0, early(j)))
    return pl.pallas_call(
        functools.partial(expand_back_kernel, tiles),
        grid=(tiles + cuts,),
        in_specs=[
            pl.BlockSpec((rows, width), lambda j: (0, 0)),
            by_unit,
            by_unit,
            pl.BlockSpec((width, tile), lambda j: (0, early(j))),
            pl.BlockSpec((2, units, width // cuts), lambda j: (0, 0, late(j))),
        ],
        out_specs=[
            by_unit,
            by_unit,
            pl.BlockSpec((cut, width // cuts), lambda j: (0, late(j))),
            pl.BlockSpec((rows - cut, width // cuts), lambda j: (0, late(j))),
        ],
        out_shape=[
            jax.ShapeDtypeStruct((rows, units), BF16),
            jax.ShapeDtypeStruct((rows, units), BF16),
            jax.ShapeDtypeStruct((cut, width), BF16),
            jax.ShapeDtypeStruct((rows - cut, width), BF16),
        ],
        scratch_shapes=[pltpu.VMEM((2 * tiles, rows, tile), BF16)],
        compiler_params=pltpu.CompilerParams(vmem_limit_bytes=VMEM_BYTES),
    )(grads, gate, upward, shrink, weight)


class Plan:
    def __init__(self, dp, fsdp):
        self.dp, self.fsdp = dp, fsdp
        self.clock = None
        self.bits = [1 << k for k in range(1, (fsdp - 1).bit_length())] + [1]
        self.short = fsdp == 8

    def tie(self, values):
        if self.clock is None:
            return tuple(values)
        return lax.optimization_barrier((tuple(values), self.clock))[0]

    def step(self, work, *values):
        found = work(*self.tie(values))
        self.clock = jax.tree.leaves(found)
        return found

    def window(self, sends, *works):
        values = self.tie([value for value, _ in sends])
        came = []
        for value, (_, mask) in zip(values, sends):
            axis, count = ("fsdp", self.fsdp) if mask > 0 else ("dp", self.dp)
            pairs = [(i, i ^ abs(mask)) for i in range(count)]
            came.append(lax.ppermute(value, axis, pairs))
        self.came = came
        gave, done = [], []
        for work in works:
            gave.append(work())
            done += self.clock
        came, self.clock = lax.optimization_barrier((came, done or came))
        return came, gave

    def wait(self, value):
        self.clock = [*self.clock, value]
        return value

    def merge(self, rows, sums, first, second):
        half = rows // 2
        beside, above = sums[rows : 2 * rows], sums[2 * rows : 3 * rows]
        return (
            jnp.concatenate([beside[:half], add_low(beside[half:], second)]),
            jnp.concatenate([add_low(above[:half], first), above[half:]]),
        )

    def spread(self, block, marks=None, works=((), (), ()), extra=None, pause=None):
        small = marks is not None
        gave, more = [], []

        def added(k):
            return [] if extra is None else extra(k, more)

        if self.short:
            half = block.shape[0] // 2
            (beside, above, other, *got), found = self.window(
                [(block, 2), (block, 4), (block, 1)] + [(marks, 2)] * small + added(0), *works[0]
            )
            gave += found
            more.append(got)
            if pause is not None:
                pause()
            if small:
                marks = self.step(lambda a, b: jnp.concatenate([a, b]), marks, *got)
            upper, lower, pair = self.step(
                lambda a, b: (a[:half], b[half:], jnp.concatenate([b, a])), above, beside
            )
            (first, second, pair, *got), found = self.window(
                [(upper, 2), (lower, 4), (pair, 1)] + [(marks, 4)] * small + added(1),
                *[functools.partial(w, [block, beside, above, other]) for w in works[1]],
            )
            gave += found
            more.append(got)
            across = self.step(lambda a, b: jnp.concatenate([a, b]), first, second)
            if small:
                marks = self.step(lambda a, b: jnp.concatenate([a, b]), marks, *got)
            near = [block, beside, above, across]
            (far, *got), found = self.window(
                [(across, 1)] + [(marks, 1)] * small + added(2),
                *[functools.partial(w, near) for w in works[2]],
            )
            more.append(got)
            size = block.shape[0]
            got = got if extra is None else more
            return near, [other, pair[:size], pair[size:], far], (marks, *got), gave + found
        near = [block]
        for bit in self.bits[:-1]:
            got, _ = self.window([(piece, bit) for piece in near] + [(marks, bit)] * small)
            if small:
                marks = jnp.concatenate([marks, got[-1]])
            near = near + got[: len(near)]
        for work in [*works[0], *([pause] if pause else []), *works[1]]:
            gave.append(work())
        got, found = self.window(
            [(piece, 1) for piece in near] + [(marks, 1)] * small,
            *[functools.partial(w, near) for w in works[2]],
        )
        return near, got[: len(near)], (marks, *got[len(near) :]), gave + found

    def settle(self, near, far, rows, works=((), (), ()), small=None, got=None, finish=None):
        gave = []

        def sends(bit):
            return [] if small is None else [(small[bit:], bit)]

        def sum_small(got, bit):
            if got:
                return self.step(lambda a, b: a[:bit] + b, small, *got)
            return None

        if not self.short:
            terms = jnp.concatenate([near(), far])
            for work in [*works[0], *works[1], *works[2]]:
                gave.append(work())
            for bit in reversed(self.bits):
                size = terms.shape[0] // 2
                if got is None:
                    (got,), _ = self.window([(terms[size:], bit)])
                terms = self.step(add_low, terms[:size], got)
                got = None
            if small is not None:
                for bit in sorted(self.bits, reverse=True):
                    small = sum_small(self.window(sends(bit))[0], bit)
            parts = terms, jnp.zeros_like(terms), jnp.zeros_like(terms)
            if finish is not None:
                finish(*parts)
            return parts, gave, small
        half = rows // 2
        if got is None:
            (got,), (near, *found) = self.window([(far, 1)], near, *works[0])
            gave += found
        else:
            near = near()
        sums = self.step(add_low, near, got)
        across = sums[3 * rows :]
        (first, second, *more), found = self.window(
            [(across[:half], 2), (across[half:], 4)] + sends(4), *works[1]
        )
        gave += found
        small = sum_small(more, 4)

        beside, above = self.step(functools.partial(self.merge, rows), sums, first, second)
        (beside, above, *more), found = self.window([(beside, 2), (above, 4)] + sends(2), *works[2])
        small = sum_small(more, 2)
        if small is not None:
            (more,), _ = self.window(sends(1), lambda: finish(sums[:rows], beside, above))
            small = sum_small([more], 1)
        return (sums[:rows], beside, above), gave + found, small

    def sum_pair(self, rows, near, across, got):
        return add_low(near[rows:], got[: 2 * rows]), add_low(across, got[2 * rows :])

    def merge_pair(self, rows, pair, first, second):
        return self.merge(rows, jnp.concatenate([pair[:rows], pair]), first, second)

    def settle_mixed(self, first, across, others, rows, works):
        half = rows // 2
        (got,), ((near, other), *gave) = self.window([(others, 1)], first, *works[0])
        pair, across = self.step(functools.partial(self.sum_pair, rows), near, across, got)
        (upper, lower, own), (_, *found) = self.window(
            [(across[:half], 2), (across[half:], 4), (other, 1)],
            lambda: self.wait(self.came[2]),
            *works[1],
        )
        gave += found
        beside, above = self.step(functools.partial(self.merge_pair, rows), pair, upper, lower)
        (beside, above), found = self.window([(beside, 2), (above, 4)], *works[2])
        return (near[:rows], own, beside, above), gave + found

    def columns_split(self, shard):
        rows, columns = shard.shape
        width = columns // (self.dp * self.fsdp)
        blocks = shard.reshape(rows, self.dp, self.fsdp, width).transpose(2, 0, 1, 3)
        return blocks.reshape(self.fsdp, rows, self.dp * width)

    def exchange(self, blocks):
        return lax.all_to_all(blocks, "fsdp", 0, 0, tiled=True)

    def columns_back(self, *sums):
        rows = sums[0].shape[0] // self.fsdp
        blocks = [value.reshape(self.fsdp, rows, -1) for value in sums]
        blocks = self.exchange(jnp.concatenate(blocks, axis=-1))
        found, last = [], 0
        for value in sums:
            first, last = last, last + value.shape[1]
            block = blocks[..., first:last].reshape(self.fsdp, rows, self.dp, -1)
            found.append(block.transpose(1, 2, 0, 3).reshape(rows, self.fsdp * value.shape[1]))
        return found


def local(
    dp,
    fsdp,
    tokens,
    positions,
    cotangent,
    entry_weight,
    mixing_weight,
    attention_gain,
    expand_weight,
    shrink_weight,
    feedforward_gain,
    entry_moment,
    entry_square,
    mixing_moment,
    mixing_square,
    attention_moment,
    attention_square,
    expand_moment,
    expand_square,
    shrink_moment,
    shrink_square,
    feedforward_moment,
    feedforward_square,
):
    plan = Plan(dp, fsdp)
    step, window, wait = plan.step, plan.window, plan.wait
    rows = tokens.shape[0]
    width = tokens.shape[1]
    group = fsdp // 2
    whole_heads = entry_weight.shape[1] == HEAD
    heads = HEADS // fsdp
    span = heads * HEAD
    factor = HEAD ** (-0.5)
    state = {}

    def work(call, *values):
        return lambda *_: step(call, *values)

    def store(name, call, *values):
        def run(*_):
            state[name] = step(call, *values)

        return run

    def low_of(value):
        return value.astype(BF16)

    join = lambda *a: jnp.concatenate(a)
    product_last = lambda a, b: contract_last(a, b).astype(BF16)
    product_plain = lambda a, b: plain_product(a, b).astype(BF16)

    attention_low = step(
        lambda a, b: jnp.concatenate([a, b]).astype(BF16), entry_weight, mixing_weight
    )
    role = lax.axis_index("fsdp")
    if whole_heads:
        attention_all = lax.all_gather(attention_low, "dp", axis=1, tiled=True)
    else:
        attention_all = lax.all_gather(attention_low, AXES, axis=1, tiled=True)

    def gains_dp(*gains):
        gains = jnp.concatenate(gains).astype(BF16)[:, None]
        return lax.all_gather(gains, "dp", axis=1, tiled=True)

    def gains_fsdp(gains):
        return lax.all_gather(gains[:, :, None], "fsdp", axis=2, tiled=True)

    def columns_work(rows_held):
        return plan.exchange(plan.columns_split(rows_held))

    spread_tokens, far_tokens, (near_places, far_places), _ = plan.spread(
        tokens,
        positions[None],
        (
            [
                store("gains_dp", gains_dp, attention_gain, feedforward_gain),
                store("expand_low", low_of, expand_weight),
            ],
            [lambda *_: state.update(gains=step(gains_fsdp, state["gains_dp"]))],
            [],
        ),
    )
    gains = state["gains"].reshape(2, width).astype(F32)
    gain_one, gain_two = gains[0], gains[1]
    expand_role = lax.all_gather(state["expand_low"], "dp", axis=1, tiled=True)

    inputs = tokens.astype(F32)
    live = (positions >= 0).astype(F32)[:, None]
    grad_out = cotangent.astype(F32) * live
    grad_low = step(low_of, grad_out)
    state["turn near"] = step(lambda a: turn_tables(a, heads), near_places)
    state["turn far"] = step(lambda a: turn_tables(a, heads), far_places)

    def attend_work(name, blocks):
        def run(*_):
            state["attend " + name] = step(
                functools.partial(attend_blocks, span),
                blocks,
                gain_one,
                state["entry"],
                *state["turn " + name],
            )

        return run

    def attention_weights():
        found = wait(attention_all)
        if whole_heads:
            state["entry"] = found.reshape(4 * span, width)
            (held,) = plan.tie([split_heads(state["entry"], dp, fsdp, span)])
            mixing_role = plan.exchange(held).reshape(fsdp, dp, HEAD, span)
            state["mixing"] = mixing_role.transpose(1, 0, 2, 3).reshape(width, span)
        else:
            own = lax.dynamic_slice_in_dim(found[:3], role * span, span, axis=1)
            state["entry"] = own.reshape(3 * span, width)
            state["mixing"] = lax.dynamic_slice_in_dim(found[3], role * span, span, axis=1)
        attend_work("far", far_tokens)()

    near_grad, far_grad, _, _ = plan.spread(
        grad_low,
        None,
        ([], [attend_work("near", spread_tokens)], []),
        pause=attention_weights,
    )
    mixing_role = wait(state["mixing"])
    entry_role = state["entry"]
    far = step(product_last, state["attend far"][2], mixing_role)
    near = work(product_last, state["attend near"][2], mixing_role)
    shrink_low = step(low_of, shrink_weight[0])
    parts, (shrink_blocks, *_), _ = plan.settle(
        near,
        far,
        rows,
        (
            [work(columns_work, shrink_low)],
            [],
            [],
        ),
    )
    shrink_role = lax.all_gather(shrink_blocks, "dp", axis=0, tiled=True).reshape(width, -1)

    def norm_middle(inputs, gain, own, beside, above):
        middle = inputs + own.astype(F32) + beside.astype(F32) + above.astype(F32)
        scale = lax.rsqrt(jnp.mean(middle * middle, axis=-1, keepdims=True) + EPS)
        return (middle * scale * gain).astype(BF16), middle, scale

    expand_role = wait(expand_role)
    low_two, middle, scale_two = step(norm_middle, inputs, gain_two, *parts)

    def grouped(near, far):
        if not plan.short:
            return near, far
        return [*near[:3], far[0]], [near[3], *far[1:]]

    first_grad, second_grad = grouped(near_grad, far_grad)

    def expand_first(blocks):
        state["up first"] = step(expand_blocks, blocks, expand_role)

    near_two, far_two, _, _ = plan.spread(
        low_two,
        None,
        (
            [store("grad first", join, *first_grad), store("grad second", join, *second_grad)],
            [expand_first] * plan.short,
            [expand_first] * (not plan.short),
        ),
    )
    state["up second"] = step(expand_blocks, grouped(near_two, far_two)[1], expand_role)
    shrink_grad = step(
        product_pairs,
        state["grad first"],
        state["up first"][3],
        state["grad second"],
        state["up second"][3],
    )
    shrink_summed = lax.psum_scatter(shrink_grad, "dp", scatter_dimension=0, tiled=True)
    shrink_role = wait(shrink_role)

    def expand_back(name, cut):
        return step(
            functools.partial(expand_back_blocks, cut * rows),
            state["grad " + name],
            *state["up " + name][1:3],
            shrink_role,
            expand_role,
        )

    second_back = expand_back("second", 1)

    def first_terms():
        state["back"] = expand_back("first", 3)
        return state["back"][2:]

    def expand_grad(index):
        return lambda *_: step(
            product_pairs,
            state["back"][index],
            state["up first"][0],
            second_back[index],
            state["up second"][0],
        )

    works = ([], [expand_grad(0)], [expand_grad(1)])
    if plan.short:
        parts, gave = plan.settle_mixed(first_terms, *second_back[2:], rows, works)
    else:
        parts, gave, _ = plan.settle(
            lambda: join(*first_terms()), join(*second_back[2:]), rows, works
        )
    gate_grad, up_grad = gave

    def output_work(name, cut):
        return store(
            "out " + name,
            functools.partial(output_blocks, cut * rows),
            state["up " + name][3],
            shrink_role,
        )

    gate_summed = lax.psum_scatter(gate_grad, "dp", scatter_dimension=0, tiled=True)
    up_summed = lax.psum_scatter(up_grad, "dp", scatter_dimension=0, tiled=True)

    shrink_summed = wait(shrink_summed)

    def expand_update(gate, up, weight, moment, square):
        gradient = jnp.stack([gate, up]).astype(F32)
        return gradient, *adamw(weight, gradient, moment, square, RATE, DECAY)

    def back_two(middle, scale, gain, grad_out, *parts):
        grad = sum(value.astype(F32) for value in parts)
        middle_back, gain_grad = norm_back(middle, scale, gain, grad)
        middle_grad = grad_out + middle_back
        return middle_grad.astype(BF16), middle_grad, gain_grad

    branch_low, middle_grad, gain_two_grad = step(
        back_two, middle, scale_two, gain_two, grad_out, *parts
    )

    def attend_back(name, grads, blocks, earlier):
        normed, joint, attended = state["attend " + name]
        return step(
            functools.partial(attend_back_blocks, span),
            grads,
            blocks,
            mixing_role,
            entry_role,
            joint,
            attended,
            normed,
            state["turn " + name],
            earlier,
        )

    def order_gains(gain_one_grad, gain_two_grad):
        gains = jnp.stack([gain_one_grad[0], gain_two_grad])
        gains = gains.reshape(2, dp, fsdp, width // (dp * fsdp)).transpose(2, 1, 0, 3)
        return jnp.take(gains, jnp.arange(fsdp) ^ role, axis=0)

    def extra_output(k, came):
        if k == 0:
            return []
        if k == 1:
            return [(state["out second"][1], 1), (state["out first"][1], 1)]
        state["sums"] = step(
            functools.partial(plan.sum_pair, rows),
            state["out first"][0],
            state["out second"][0],
            came[1][0],
        )
        across = state["sums"][1]
        return [(across[: rows // 2], 2), (across[rows // 2 :], 4)]

    def back_near(near_branch):
        state["near back"] = attend_back("near", near_branch, spread_tokens, [])

    def back_far():
        state["far back"] = attend_back(
            "far", far_branch, far_tokens, state["near back"][1:]
        )

    _, far_branch, came, _ = plan.spread(
        branch_low,
        None,
        (
            [output_work("second", 1), output_work("first", 3)],
            [],
            [back_near],
        ),
        extra_output,
    )
    if plan.short:
        beside, above = step(
            functools.partial(plan.merge_pair, rows), state["sums"][0], *came[3]
        )
        parts, _ = window([(beside, 2), (above, 4)], back_far)
        parts = [state["out first"][0][:rows], came[2][1], *parts]
    else:
        parts, _, _ = plan.settle(
            lambda: join(*state["out first"]),
            join(*state["out second"]),
            rows,
            ([], [back_far], []),
        )
    layer_output = step(
        lambda *a: sum((value.astype(F32) for value in a[1:]), a[0]).astype(BF16), middle, *parts
    )
    near, far = state["near back"][0], state["far back"][0]
    gate_summed = wait(gate_summed)
    up_summed = wait(up_summed)

    _, entry_grad, mixing_grad, gain_grad = state["far back"]
    mixing_grad = step(lambda a: a.T, mixing_grad)
    if whole_heads:
        mixing_summed = lax.psum_scatter(mixing_grad, "dp", scatter_dimension=0, tiled=True)
        entry_gradient = lax.psum_scatter(
            entry_grad.reshape(3, dp * HEAD, width), "dp", scatter_dimension=1, tiled=True
        )
    else:
        entry_full = lax.dynamic_update_slice_in_dim(
            jnp.zeros((3, width, width), BF16),
            entry_grad.reshape(3, span, width),
            role * span,
            axis=1,
        )
        mixing_full = lax.dynamic_update_slice_in_dim(
            jnp.zeros((width, width), BF16), mixing_grad, role * span, axis=1
        )
        entry_gradient = lax.psum_scatter(entry_full, AXES, scatter_dimension=1, tiled=True)
        mixing_summed = lax.psum_scatter(mixing_full, AXES, scatter_dimension=0, tiled=True)

    gains = step(order_gains, gain_grad, gain_two_grad)
    (got,), ((shrink_back,),) = window([(far, 1)], work(plan.columns_back, shrink_summed))

    def back_input(inputs, gain, middle_grad, *parts):
        scale = lax.rsqrt(jnp.mean(inputs * inputs, axis=-1, keepdims=True) + EPS)
        grad = sum(value.astype(F32) for value in parts)
        return middle_grad + norm_back(inputs, scale, gain, grad)[0]

    def finish(*parts):
        state["input"] = step(back_input, inputs, gain_one, middle_grad, *parts)

    def columns_update(shrink_back, mixing_summed, shrink, mixing):
        if whole_heads:
            (mixing_summed,) = plan.columns_back(mixing_summed)
        found = []
        for gradient, values, rate in (
            (shrink_back, shrink, RATE),
            (mixing_summed, mixing, MIXING_RATE),
        ):
            gradient = gradient[None].astype(F32)
            found.append((gradient, adamw(values[0], gradient, *values[1:], rate, DECAY)))
        return found

    _, _, gains = plan.settle(
        lambda: near,
        far,
        rows,
        (
            [],
            [
                store(
                    "expand",
                    expand_update,
                    gate_summed,
                    up_summed,
                    expand_weight,
                    expand_moment,
                    expand_square,
                )
            ],
            [
                store(
                    "columns",
                    columns_update,
                    shrink_back,
                    mixing_summed,
                    (shrink_weight, shrink_moment, shrink_square),
                    (mixing_weight, mixing_moment, mixing_square),
                )
            ],
        ),
        gains,
        got,
        finish,
    )
    input_gradient = state["input"]
    def order_dp(gains):
        return jnp.take(gains[0], jnp.arange(dp) ^ lax.axis_index("dp"), axis=0)

    gains = step(order_dp, gains)
    for bit in reversed([1 << k for k in range((dp - 1).bit_length())]):
        (got,), _ = window([(gains[bit:], -bit)])
        gains = step(lambda a, b: a[:bit] + b, gains, got)
    gain_grads = gains[0]
    attention_gradient, feedforward_gradient = gain_grads[:1], gain_grads[1:]
    (shrink_gradient, shrink_new), (mixing_gradient, mixing_new) = state["columns"]
    expand_gradient, *expand_new = state["expand"]
    entry_gradient = entry_gradient.astype(F32)
    entry_new = adamw(entry_weight, entry_gradient, entry_moment, entry_square, RATE, DECAY)
    attention_new = adamw(
        attention_gain, attention_gradient, attention_moment, attention_square, GAIN_RATE, 0.0
    )
    feedforward_new = adamw(
        feedforward_gain,
        feedforward_gradient,
        feedforward_moment,
        feedforward_square,
        GAIN_RATE,
        0.0,
    )
    return (
        layer_output,
        input_gradient,
        entry_gradient,
        mixing_gradient,
        attention_gradient,
        expand_gradient,
        shrink_gradient,
        feedforward_gradient,
        entry_new[0],
        mixing_new[0],
        attention_new[0],
        expand_new[0],
        shrink_new[0],
        feedforward_new[0],
        entry_new[1],
        entry_new[2],
        mixing_new[1],
        mixing_new[2],
        attention_new[1],
        attention_new[2],
        expand_new[1],
        expand_new[2],
        shrink_new[1],
        shrink_new[2],
        feedforward_new[1],
        feedforward_new[2],
    )


def solution(mesh):
    placed = (
        P(("dp", "fsdp"), None),
        P(("dp", "fsdp")),
        P(("dp", "fsdp"), None),
        P(None, ("dp", "fsdp"), None),
        P(None, ("dp", "fsdp"), None),
        P(None, ("dp", "fsdp")),
        P(None, ("dp", "fsdp"), None),
        P(None, ("dp", "fsdp"), None),
        P(None, ("dp", "fsdp")),
        P(None, ("dp", "fsdp"), None),
        P(None, ("dp", "fsdp"), None),
        P(None, ("dp", "fsdp"), None),
        P(None, ("dp", "fsdp"), None),
        P(None, ("dp", "fsdp")),
        P(None, ("dp", "fsdp")),
        P(None, ("dp", "fsdp"), None),
        P(None, ("dp", "fsdp"), None),
        P(None, ("dp", "fsdp"), None),
        P(None, ("dp", "fsdp"), None),
        P(None, ("dp", "fsdp")),
        P(None, ("dp", "fsdp")),
    )
    return jax.shard_map(
        functools.partial(local, mesh.shape["dp"], mesh.shape["fsdp"]),
        mesh=mesh,
        in_specs=placed,
        out_specs=(
            P(("dp", "fsdp"), None),
            P(("dp", "fsdp"), None),
            P(None, ("dp", "fsdp"), None),
            P(None, ("dp", "fsdp"), None),
            P(None, ("dp", "fsdp")),
            P(None, ("dp", "fsdp"), None),
            P(None, ("dp", "fsdp"), None),
            P(None, ("dp", "fsdp")),
            P(None, ("dp", "fsdp"), None),
            P(None, ("dp", "fsdp"), None),
            P(None, ("dp", "fsdp")),
            P(None, ("dp", "fsdp"), None),
            P(None, ("dp", "fsdp"), None),
            P(None, ("dp", "fsdp")),
            P(None, ("dp", "fsdp"), None),
            P(None, ("dp", "fsdp"), None),
            P(None, ("dp", "fsdp"), None),
            P(None, ("dp", "fsdp"), None),
            P(None, ("dp", "fsdp")),
            P(None, ("dp", "fsdp")),
            P(None, ("dp", "fsdp"), None),
            P(None, ("dp", "fsdp"), None),
            P(None, ("dp", "fsdp"), None),
            P(None, ("dp", "fsdp"), None),
            P(None, ("dp", "fsdp")),
            P(None, ("dp", "fsdp")),
        ),
        check_vma=False,
    )
```
